32 devices in a mesh: level: 4 (over x, core), band: 8 (over z, y).
Axes of the slice: x: 2, y: 2, z: 4, core: 2. Of those that a mesh axis runs over, the one named last changes fastest.
Arguments:
- features: bfloat16 [16384, 128], P('band'), may hold values from -6 to 6
- block_perm: int32 [4, 8, 8], P('level', 'band'), may hold values from 0 to 7, each once within a row
- tile_rows: int32 [4, 288], P('level', 'band'), may hold values from 0 to 63, as said below
- tile_cols: int32 [4, 288], P('level', 'band'), may hold values from 0 to 63, as said below
- tile_vals: bfloat16 [4, 288, 256, 256], P('level', 'band'), may hold values from -0.1875 to 0.1875
Outputs:
- forward: bfloat16 [8, 2048, 128], P('band', 'level')
- backward: bfloat16 [8, 2048, 128], P('band', 'level')
The draws below stay inside these ranges and needn't reach their ends.
Inputs may be any that keep to these rules, and one draw needn't show every extreme that they name: `block_perm`: each band device's 8 entries of a level are a permutation of 0 to 7. `tile_rows`: the 36 tiles stored at band index b of a level each have either block row in b's blocks [b * 8, (b + 1) * 8) and block column in the blocks of band indices b - 1, b, b + 1 or below 2, or block row below 2 and block column in b's blocks; positions may repeat. `tile_cols`: as for tile_rows, paired entry by entry.
All inputs are finite; a program needn't handle non-finite values.
Results may differ from the reference program's by a relative error of at most 0.001.
Values may be sent and summed in bfloat16 or wider, within the bound.
No kernel may reach another device: no remote copies, remote signals or barrier semaphores. Data moves between devices by JAX's collectives and lax.ppermute only.
A program may use at most 128 MiB of HBM per device.

```python
import jax
import jax.numpy as jnp

F = 128
TILE = 256
RDEV = 2048
K = 36
HEADB = 2
RB = 8
NBLK = 64
NROWS = 16384
N_LEVEL = 4
N_BAND = 8


def tile_layout(key):
    key = jax.random.fold_in(key, 7)
    keys = jax.random.split(key, 6)
    shape = (N_LEVEL, N_BAND * K)
    flat = jnp.arange(N_BAND * K, dtype=jnp.int32)
    band_of = jnp.broadcast_to(flat // K, shape)
    slot = jnp.broadcast_to(flat % K, shape)
    own_row = band_of * RB + jax.random.randint(keys[0], shape, 0, RB)
    own_col = band_of * RB + jax.random.randint(keys[1], shape, 0, RB)
    steps_near = jax.random.randint(keys[2], shape, -1, 2)
    near_band = jnp.clip(band_of + steps_near, 0, N_BAND - 1)
    near_col = near_band * RB + jax.random.randint(keys[3], shape, 0, RB)
    head_pick = jax.random.randint(keys[4], shape, 0, HEADB)
    row_head = slot < K // 6
    col_head = (slot >= K // 6) & (slot < K // 3)
    rows = jnp.where(row_head, head_pick, own_row)
    cols = jnp.where(row_head, own_col, jnp.where(col_head, head_pick, near_col))
    rows = jnp.where(slot == 0, 0, rows)
    last_row = band_of * RB + RB - 1
    last_col = jnp.minimum(band_of + 1, N_BAND - 1) * RB + RB - 1
    rows = jnp.where(slot == K - 1, last_row, rows)
    cols = jnp.where(slot == K - 1, last_col, cols)
    scores = jax.random.randint(keys[5], (N_LEVEL, N_BAND, K), 0, 1 << 20) * K + jnp.arange(K, dtype=jnp.int32)
    slot_order = jnp.argsort(scores, axis=-1, stable=True)
    rows = jnp.take_along_axis(rows.reshape(N_LEVEL, N_BAND, K), slot_order, axis=-1).reshape(shape)
    cols = jnp.take_along_axis(cols.reshape(N_LEVEL, N_BAND, K), slot_order, axis=-1).reshape(shape)
    return (rows.astype(jnp.int32), cols.astype(jnp.int32))


def draw_tile_rows(key, part):
    return tile_layout(key)[0]


def draw_tile_cols(key, part):
    return tile_layout(key)[1]


def level_of(own_key, extent, cuts, low, largest):
    level = 1.0
    for position, parts in cuts:
        heights = jax.random.uniform(jax.random.fold_in(jax.random.fold_in(own_key, 6), position), (parts,), jnp.float32, low / len(cuts), largest / len(cuts))
        level = level * jnp.repeat(jnp.exp(heights), extent[position] // parts).reshape((-1,) + (1,) * (len(extent) - 1 - position))
    return level


def scatter_about(rng, shape, scale, reach, cuts=(), held_as=jnp.bfloat16):
    level = level_of(rng, shape, cuts, -0.22, 0.18) if cuts else 1.0
    values = jax.random.normal(rng, shape, jnp.float32) * scale * level
    return jnp.minimum(jnp.maximum(values, -reach), reach).astype(held_as)


def setup_inputs(seed: int = 0) -> dict:
    arg_keys = jax.random.split(jax.random.key(seed), 6)
    return {
        "features": scatter_about(arg_keys[0], (NROWS, F), 1.0, 6.0, ((0, 8),)),
        "block_perm": jax.vmap(lambda own: jax.random.permutation(own, RB))(jax.random.split(arg_keys[1], N_LEVEL * N_BAND)).reshape((N_LEVEL, N_BAND, RB)).astype(jnp.int32),
        "tile_rows": draw_tile_rows(jax.random.fold_in(arg_keys[5], 71), 0),
        "tile_cols": draw_tile_cols(jax.random.fold_in(arg_keys[5], 71), 0),
        "tile_vals": scatter_about(arg_keys[4], (N_LEVEL, NBLK * K // RB, TILE, TILE), (TILE * K // RB) ** -0.5, 0.1875, ((0, 4), (1, 8))),
    }


def reference(features, block_perm, tile_rows, tile_cols, tile_vals):
    x_blocks = features.reshape(NBLK, TILE, F).astype(jnp.float32)
    fwd = jnp.zeros((NBLK, TILE, F), jnp.float32)
    bwd = jnp.zeros((NBLK, TILE, F), jnp.float32)
    for level_id in range(N_LEVEL):
        global_of = (jnp.arange(N_BAND, dtype=jnp.int32)[:, None] * RB + block_perm[level_id].astype(jnp.int32)).reshape(-1)
        level_x = x_blocks[global_of]
        rows = tile_rows[level_id].astype(jnp.int32)
        cols = tile_cols[level_id].astype(jnp.int32)
        vals = tile_vals[level_id].astype(jnp.float32)
        prod_fwd = jnp.einsum("kij,kjf->kif", vals, level_x[cols])
        prod_bwd = jnp.einsum("kij,kif->kjf", vals, level_x[rows])
        level_fwd = jax.ops.segment_sum(prod_fwd, rows, num_segments=NBLK)
        level_bwd = jax.ops.segment_sum(prod_bwd, cols, num_segments=NBLK)
        fwd = fwd.at[global_of].add(level_fwd)
        bwd = bwd.at[global_of].add(level_bwd)
    forward = fwd.reshape(N_BAND, RDEV, F).astype(jnp.bfloat16)
    backward = bwd.reshape(N_BAND, RDEV, F).astype(jnp.bfloat16)
    return forward, backward
```

```python
import functools

import jax
import jax.numpy as jnp
from jax import lax
from jax.experimental import pallas as pl
from jax.experimental.pallas import tpu as pltpu
from jax.sharding import PartitionSpec as P

HEADB = 2
GROUPS = 16
UNROLL = 4
F32 = jnp.float32
I16 = jnp.int16
VMEM = pl.BlockSpec(memory_space=pltpu.VMEM)
SMEM = pl.BlockSpec(memory_space=pltpu.SMEM)


def call(kernel, outs, ins, scratch=(), flops=0):
    bytes_moved = sum(a.size * a.dtype.itemsize for a in (*outs, *ins))
    return pl.pallas_call(
        kernel,
        out_shape=outs,
        in_specs=[SMEM if a.ndim == 1 else VMEM for a in ins],
        out_specs=[VMEM] * len(outs),
        scratch_shapes=list(scratch),
        compiler_params=pltpu.CompilerParams(vmem_limit_bytes=32 * 2**20),
        cost_estimate=pl.CostEstimate(flops=flops, bytes_accessed=bytes_moved, transcendentals=0),
    )(*ins)


def array(shape, dtype=F32):
    return jax.ShapeDtypeStruct(tuple(shape), dtype)


def encode(value):
    rows, width = value.shape
    grouped = value.reshape(GROUPS, rows // GROUPS, width)
    largest = jnp.maximum(jnp.max(jnp.abs(grouped), axis=1), 1e-30)
    power = jnp.ceil(jnp.log2(largest))
    scaled = jnp.round(grouped * jnp.exp2(15.0 - power)[:, None, :])
    codes = jnp.clip(scaled, -32767.0, 32767.0).astype(jnp.int32).astype(I16)
    return codes.reshape(rows, width), power.astype(jnp.int32).astype(I16)


def put_coded(ref, index, value):
    rows = value.shape[0]
    codes, power = encode(value)
    ref[index, :rows, :] = codes
    ref[index, rows:, :] = power


def get_coded(ref, index):
    rows, width = ref.shape[-2] - GROUPS, ref.shape[-1]
    codes = ref[index, :rows, :].astype(jnp.int32).astype(F32)
    power = ref[index, rows:, :].astype(jnp.int32).astype(F32)
    grouped = codes.reshape(GROUPS, rows // GROUPS, width) * jnp.exp2(power - 15.0)[:, None, :]
    return grouped.reshape(rows, width)


def dot(a, b):
    return jnp.dot(a, b, preferred_element_type=F32)


def dot_t(a, b):
    return lax.dot_general(a, b, (((0,), (0,)), ((), ())), preferred_element_type=F32)


class Meta:
    def __init__(self, ref, count, blocks):
        self.ref, self.count, self.blocks = ref, count, blocks
        self.level = ref[2 * count + blocks]
        self.band = ref[2 * count + blocks + 1]

    def row(self, k):
        return self.ref[k]

    def col(self, k):
        return self.ref[self.count + k]

    def perm(self, j):
        return self.ref[2 * self.count + j]

    def low(self):
        return self.band * self.blocks

    def own_row(self, k):
        at = self.row(k) - self.low()
        return (at >= 0) & (at < self.blocks)

    def own_col(self, k):
        at = self.col(k) - self.low()
        return (at >= 0) & (at < self.blocks)

    def near_col(self, k):
        at = self.col(k) - self.low()
        return (at >= -self.blocks) & (at < 2 * self.blocks)

    def x_row(self, k):
        return self.perm(self.row(k) - self.low())

    def x_col(self, k):
        return self.perm(self.col(k) - self.low())


def for_tiles(count, chosen, listed, product, place, acc, trash):
    def note(k, n):
        listed[n] = k
        return n + chosen(k).astype(jnp.int32)

    n = lax.fori_loop(0, count, note, jnp.int32(0))
    unit = acc.shape[1]

    def step(i, carry):
        tiles = [listed[jnp.minimum(i * UNROLL + u, n - 1)] for u in range(UNROLL)]
        products = [product(k) for k in tiles]
        for u in range(UNROLL):
            real = i * UNROLL + u < n
            for part in range(products[u].shape[0] // unit):
                slot = jnp.where(real, place(tiles[u], part), trash)
                acc[slot] += products[u][part * unit : (part + 1) * unit]
        return carry

    lax.fori_loop(0, lax.div(n + UNROLL - 1, jnp.int32(UNROLL)), step, 0)


class Shares:
    def __init__(self, levels, rdev, tile, parts):
        self.share = rdev // levels
        self.unit = min(tile, self.share)
        self.per = self.share // self.unit
        self.m = levels // 2
        self.parts = parts
        self.tile = tile
        self.slots = 2 * parts * self.m * self.per

    def slot(self, level, part, block, piece):
        at = (block * self.tile + piece * self.unit) // self.unit
        owner = lax.div(at, jnp.int32(self.per))
        keep = 1 - ((owner ^ level) & 1)
        return ((keep * self.parts + part) * self.m + (owner >> 1)) * self.per + lax.rem(at, jnp.int32(self.per))


def heads_out_kernel(count, blocks, meta_ref, x, vals, coded, plain, acc, listed):
    meta = Meta(meta_ref, count, blocks)
    acc[...] = jnp.zeros_like(acc)
    for_tiles(
        count,
        lambda k: ~meta.own_row(k),
        listed,
        lambda k: dot(vals[k], x[meta.x_col(k)]),
        lambda k, part: meta.row(k),
        acc,
        2 * HEADB,
    )
    for_tiles(
        count,
        lambda k: meta.own_row(k) & ~meta.near_col(k),
        listed,
        lambda k: dot_t(vals[k], x[meta.x_row(k)]),
        lambda k, part: HEADB + meta.col(k),
        acc,
        2 * HEADB,
    )
    for i in range(2 * HEADB):
        plain[i] = acc[i]
        put_coded(coded, i, acc[i])


def heads_add_kernel(had, came, coded, plain):
    for i in range(had.shape[0]):
        value = had[i] + get_coded(came, i)
        plain[i] = value
        put_coded(coded, i, value)


def halo_out_kernel(count, blocks, shares, meta_ref, near_ref, x, vals, send, keep, own, acc, listed):
    meta = Meta(meta_ref, count, blocks)
    acc[...] = jnp.zeros_like(acc)
    trash = 2 * shares.slots

    def place(k, piece):
        at = meta.col(k) - meta.low()
        is_low, is_high = at < 0, at >= blocks
        block = jnp.where(
            is_low,
            near_ref[jnp.clip(at + blocks, 0, blocks - 1)],
            jnp.where(
                is_high,
                near_ref[blocks + jnp.clip(at - blocks, 0, blocks - 1)],
                meta.perm(jnp.clip(at, 0, blocks - 1)),
            ),
        )
        part = jnp.where(is_low | is_high, is_high.astype(jnp.int32), 1)
        base = jnp.where(is_low | is_high, 0, shares.slots)
        return base + shares.slot(meta.level, part, block, piece)

    for_tiles(
        count,
        lambda k: meta.own_row(k) & meta.near_col(k),
        listed,
        lambda k: dot_t(vals[k], x[meta.x_row(k)]),
        place,
        acc,
        trash,
    )
    for_tiles(
        count,
        lambda k: meta.own_row(k) & meta.own_col(k),
        listed,
        lambda k: dot(vals[k], x[meta.x_col(k)]),
        lambda k, piece: shares.slots + shares.slot(meta.level, 0, meta.x_row(k), piece),
        acc,
        trash,
    )
    half = shares.slots // 2
    send[...] = acc[:half].reshape(send.shape)
    keep[...] = acc[half : 2 * half].reshape(keep.shape)
    own[...] = acc[2 * half : 4 * half]


def own_kernel(count, blocks, shares, meta_ref, near_ref, vals, own, low, high, low2, high2, xh, heads, send, keep, acc, xw, listed):
    meta = Meta(meta_ref, count, blocks)
    half_blocks = blocks // 2
    core = meta.level & 1
    for j in range(half_blocks):
        xw[core * half_blocks + j] = low[j]
        xw[(1 - core) * half_blocks + j] = low2[j]
        xw[blocks + core * half_blocks + j] = high[j]
        xw[blocks + (1 - core) * half_blocks + j] = high2[j]
    for j in range(HEADB):
        xw[2 * blocks + j] = xh[j]
    acc[: shares.slots] = own[...]
    trash = shares.slots

    def source(k):
        at = meta.col(k) - meta.low()
        is_low = (at < 0) & (at >= -blocks)
        is_high = (at >= blocks) & (at < 2 * blocks)
        return jnp.where(
            is_low,
            near_ref[jnp.clip(at + blocks, 0, blocks - 1)],
            jnp.where(
                is_high,
                blocks + near_ref[blocks + jnp.clip(at - blocks, 0, blocks - 1)],
                2 * blocks + jnp.clip(meta.col(k), 0, HEADB - 1),
            ),
        )

    for_tiles(
        count,
        lambda k: meta.own_row(k) & ~meta.own_col(k),
        listed,
        lambda k: dot(vals[k], xw[source(k)]),
        lambda k, piece: shares.slot(meta.level, 0, meta.x_row(k), piece),
        acc,
        trash,
    )
    for_tiles(
        count,
        lambda k: ~meta.own_row(k),
        listed,
        lambda k: dot_t(vals[k], xw[2 * blocks + meta.row(k)]),
        lambda k, piece: shares.slot(meta.level, 1, meta.x_col(k), piece),
        acc,
        trash,
    )

    @pl.when(meta.band == 0)
    def _():
        for part in range(2):
            for h in range(HEADB):
                for piece in range(shares.tile // shares.unit):
                    slot = shares.slot(meta.level, part, meta.perm(h), piece)
                    acc[slot] += heads[part * HEADB + h, piece * shares.unit : (piece + 1) * shares.unit]

    half = shares.slots // 2
    send[...] = acc[:half].reshape(send.shape)
    keep[...] = acc[half : 2 * half].reshape(keep.shape)


def split_kernel(bit, coded_in, meta_ref, had, came, send, keep, at):
    mine = (meta_ref[at] >> bit) & 1
    parts, m, share, width = had.shape
    for part in range(parts):
        for i in range(m // 2):
            for half in range(2):
                j = 2 * i + (mine if half else 1 - mine)
                came_value = get_coded(came, part * m + j) if coded_in else came[part, j]
                value = had[part, j] + came_value
                if half:
                    keep[part, i] = value
                else:
                    put_coded(send, part * (m // 2) + i, value)


def edge_kernel(coded_in, had, came, low, high):
    for part, out in enumerate((low, high)):
        came_value = get_coded(came, part) if coded_in else came[part, 0]
        put_coded(out, 0, had[part, 0] + came_value)


def last_kernel(coded_in, had, came, from_low, from_high, forward, backward):
    came_values = [get_coded(came, part) if coded_in else came[part, 0] for part in range(2)]
    forward[0] = (had[0, 0] + came_values[0]).astype(forward.dtype)
    total = had[1, 0] + came_values[1] + get_coded(from_low, 0) + get_coded(from_high, 0)
    backward[0] = total.astype(backward.dtype)


def over_levels(send, keep, meta, level_at, levels):
    bit, coded = 0, False
    parts, m, share, width = keep.shape
    while True:
        pairs = [(i, i ^ (1 << bit)) for i in range(levels)]
        came = lax.ppermute(send, "level", pairs)
        if m == 1:
            return keep, came, coded
        bit += 1
        send, keep = call(
            functools.partial(split_kernel_at, bit, coded, level_at),
            (array((parts * (m // 2), share + GROUPS, width), I16), array((parts, m // 2, share, width))),
            (meta, keep, came),
        )
        coded = True
        m //= 2


def split_kernel_at(bit, coded, at, meta_ref, had, came, send, keep):
    split_kernel(bit, coded, meta_ref, had, came, send, keep, at)


def on_device(features, block_perm, tile_rows, tile_cols, tile_vals):
    rdev, width = features.shape
    blocks = block_perm.shape[2]
    tile = tile_vals.shape[2]
    count = tile_vals.shape[1]
    levels = lax.axis_size("level")
    bands = lax.axis_size("band")
    level, band = lax.axis_index("level"), lax.axis_index("band")
    up = [(i, i + 1) for i in range(bands - 1)]
    down = [(i + 1, i) for i in range(bands - 1)]
    shares = Shares(levels, rdev, tile, 2)
    share, m, unit = shares.share, shares.m, shares.unit
    level_at = 2 * count + blocks

    perm = block_perm[0, 0]
    vals = tile_vals[0]
    x = features.reshape(blocks, tile, width)
    place = jnp.stack([level, band]).astype(jnp.int32)
    meta = jnp.concatenate([tile_rows[0], tile_cols[0], perm, place])
    near = jnp.concatenate([lax.ppermute(perm, "band", up), lax.ppermute(perm, "band", down)])

    mine = lax.dynamic_slice_in_dim(x, (level & 1) * (blocks // 2), blocks // 2, 0)
    low = lax.ppermute(mine, "band", up)
    high = lax.ppermute(mine, "band", down)
    cores = [(i, i ^ 1) for i in range(levels)]
    low2 = lax.ppermute(low, "level", cores)
    high2 = lax.ppermute(high, "level", cores)

    xh = jnp.concatenate([lax.dynamic_slice_in_dim(x, perm[h], 1, 0) for h in range(HEADB)])
    step = bands // 2
    while step:
        got = lax.ppermute(xh, "band", [(i, i + step) for i in range(0, bands, 2 * step)])
        xh = jnp.where(band % (2 * step) == step, got, xh)
        step //= 2

    coded_heads = array((2 * HEADB, tile + GROUPS, width), I16)
    plain_heads = array((2 * HEADB, tile, width))
    coded, heads = call(
        functools.partial(heads_out_kernel, count, blocks),
        (coded_heads, plain_heads),
        (meta, x, vals),
        (pltpu.VMEM((2 * HEADB + 1, tile, width), F32), pltpu.SMEM((count + 1,), jnp.int32)),
    )
    step = 1
    while step < bands:
        came = lax.ppermute(coded, "band", [(i + step, i) for i in range(0, bands, 2 * step)])
        coded, heads = call(heads_add_kernel, (coded_heads, plain_heads), (heads, came))
        step *= 2

    half_shape = array((2, m, share, width))
    send, keep, own = call(
        functools.partial(halo_out_kernel, count, blocks, shares),
        (half_shape, half_shape, array((shares.slots, unit, width))),
        (meta, near, x, vals),
        (pltpu.VMEM((2 * shares.slots + 1, unit, width), F32), pltpu.SMEM((count + 1,), jnp.int32)),
    )
    had, came, was_coded = over_levels(send, keep, meta, level_at, levels)
    edge = array((1, share + GROUPS, width), I16)
    to_low, to_high = call(functools.partial(edge_kernel, was_coded), (edge, edge), (had, came))
    from_low = lax.ppermute(to_high, "band", up)
    from_high = lax.ppermute(to_low, "band", down)

    send, keep = call(
        functools.partial(own_kernel, count, blocks, shares),
        (half_shape, half_shape),
        (meta, near, vals, own, low, high, low2, high2, xh, heads),
        (
            pltpu.VMEM((shares.slots + 1, unit, width), F32),
            pltpu.VMEM((2 * blocks + HEADB, tile, width), features.dtype),
            pltpu.SMEM((count + 1,), jnp.int32),
        ),
    )
    had, came, was_coded = over_levels(send, keep, meta, level_at, levels)
    out = array((1, share, width), jnp.bfloat16)
    forward, backward = call(
        functools.partial(last_kernel, was_coded), (out, out), (had, came, from_low, from_high)
    )
    return forward, backward


def solution(mesh):
    return jax.shard_map(
        on_device,
        mesh=mesh,
        in_specs=(
            P("band", None),
            P("level", "band", None),
            P("level", "band"),
            P("level", "band"),
            P("level", "band", None, None),
        ),
        out_specs=(P("band", "level", None), P("band", "level", None)),
        check_vma=False,
    )
```

```python
import functools
import math

import jax
import jax.numpy as jnp
from jax import lax
from jax.experimental import pallas as pl
from jax.experimental.pallas import tpu as pltpu
from jax.sharding import PartitionSpec as P

HEADB = 2
GROUPS = 16
UNROLL = 4
VMEM_LIMIT = 24 * 2**20
F32 = jnp.float32
I16 = jnp.int16
VMEM = pl.BlockSpec(memory_space=pltpu.VMEM)
ANY = pl.BlockSpec(memory_space=pl.ANY)
HBM = pl.BlockSpec(memory_space=pltpu.HBM)
SMEM = pl.BlockSpec(memory_space=pltpu.SMEM)


def call(kernel, outs, ins, scratch=(), after=(), in_hbm=0):
    bytes_moved = sum(math.prod(a.shape) * a.dtype.itemsize for a in (*outs, *ins))

    def body(*refs):
        kernel(*refs[: len(ins)], *refs[len(ins) + len(after) :])

    return pl.pallas_call(
        body,
        out_shape=outs,
        in_specs=[HBM] * in_hbm + [SMEM if a.ndim == 1 else VMEM for a in ins[in_hbm:]] + [ANY] * len(after),
        out_specs=[SMEM if len(a.shape) == 1 else VMEM for a in outs],
        scratch_shapes=list(scratch),
        compiler_params=pltpu.CompilerParams(vmem_limit_bytes=VMEM_LIMIT),
        cost_estimate=pl.CostEstimate(flops=0, bytes_accessed=bytes_moved, transcendentals=0),
    )(*ins, *after)


def array(shape, dtype=F32):
    return jax.ShapeDtypeStruct(tuple(shape), dtype)


def encode(value):
    rows, width = value.shape
    grouped = value.reshape(GROUPS, rows // GROUPS, width)
    largest = jnp.maximum(jnp.max(jnp.abs(grouped), axis=1), 1e-30)
    power = jnp.ceil(jnp.log2(largest))
    scaled = jnp.round(grouped * jnp.exp2(15.0 - power)[:, None, :])
    codes = jnp.clip(scaled, -32767.0, 32767.0).astype(jnp.int32).astype(I16)
    return codes.reshape(rows, width), power.astype(jnp.int32).astype(I16)


def put_coded(ref, index, value):
    rows = value.shape[0]
    codes, power = encode(value)
    ref[index, :rows, :] = codes
    ref[index, rows:, :] = power


def get_coded(ref, index):
    rows, width = ref.shape[-2] - GROUPS, ref.shape[-1]
    codes = ref[index, :rows, :].astype(jnp.int32).astype(F32)
    power = ref[index, rows:, :].astype(jnp.int32).astype(F32)
    grouped = codes.reshape(GROUPS, rows // GROUPS, width) * jnp.exp2(power - 15.0)[:, None, :]
    return grouped.reshape(rows, width)


def dot(a, b):
    return jnp.dot(a, b, preferred_element_type=F32)


def dot_t(a, b):
    return lax.dot_general(a, b, (((0,), (0,)), ((), ())), preferred_element_type=F32)


HEAD_ROW, HEAD_COL, NEAR, OWN, REMOTE = range(5)


def packed(k, source, target):
    return k | (source << 8) | (target << 16)


def write_plan(count, blocks, rows, cols, perm, plan):
    low = lax.axis_index("band") * blocks
    n = [jnp.int32(0)] * 5
    for k in range(count):
        row, col = rows[0, k] - low, cols[0, k] - low
        own_row = (row >= 0) & (row < blocks)
        own_col = (col >= 0) & (col < blocks)
        near = (col >= -blocks) & (col < 2 * blocks)
        x_row = perm[0, 0, jnp.clip(row, 0, blocks - 1)]
        x_col = perm[0, 0, jnp.clip(col, 0, blocks - 1)]
        near_at = jnp.where(near, col + blocks, 3 * blocks + cols[0, k])
        for which, chosen, source, target in (
            (HEAD_ROW, ~own_row, x_col, rows[0, k]),
            (HEAD_COL, own_row & ~near, x_row, HEADB + cols[0, k]),
            (NEAR, own_row & near & ~own_col, x_row, near_at),
            (OWN, own_row & own_col, x_row, x_col),
            (REMOTE, own_row & ~own_col, near_at, x_row),
        ):
            plan[which * count + n[which]] = packed(k, source, target)
            n[which] = n[which] + chosen.astype(jnp.int32)
    for which in range(5):
        plan[5 * count + which] = n[which]


def for_tiles(count, plan, vals, which, jobs, acc, trash):
    n = plan[5 * count + which]
    unit = acc.shape[1]

    def step(i, carry):
        entries = []
        for u in range(UNROLL):
            real = i * UNROLL + u < n
            e = plan[which * count + jnp.minimum(i * UNROLL + u, n - 1)]
            entries.append((real, e & 255, (e >> 8) & 255, e >> 16))
        products = [[product(vals[k], s, t) for product, _ in jobs] for _, k, s, t in entries]
        for values, (real, _, s, t) in zip(products, entries):
            for value, (_, place) in zip(values, jobs):
                for piece in range(value.shape[0] // unit):
                    slot = jnp.where(real, place(s, t, piece), trash)
                    acc[slot] += value[piece * unit : (piece + 1) * unit]
        return carry

    lax.fori_loop(0, (n + UNROLL - 1) // UNROLL, step, 0)


class Shares:
    def __init__(self, levels, rdev, tile, parts):
        self.share = rdev // levels
        self.unit = min(tile, self.share)
        self.per = self.share // self.unit
        self.m = levels // 2
        self.parts = parts
        self.tile = tile
        self.pieces = tile // self.unit
        self.slots = 2 * parts * self.m * self.per

    def slot(self, part, block, piece):
        at = block * self.pieces + piece
        owner = at // self.per
        keep = 1 - ((owner ^ lax.axis_index("level")) & 1)
        return ((keep * self.parts + part) * self.m + (owner >> 1)) * self.per + at % self.per


def sides(band):
    odd = band & 1
    return 1 - odd, odd


def heads_out_kernel(count, blocks, rows_hbm, cols_hbm, perm_hbm, x_hbm, vals_hbm, plan, coded, plain, head_x, mine, x, vals, acc, rows, cols, perm, few):
    copies = [
        pltpu.make_async_copy(a, b, few.at[i])
        for i, (a, b) in enumerate(((rows_hbm, rows), (cols_hbm, cols), (perm_hbm, perm), (x_hbm, x), (vals_hbm, vals)))
    ]
    for copy in copies:
        copy.start()
    acc[...] = jnp.zeros_like(acc)
    for copy in copies[:3]:
        copy.wait()
    write_plan(count, blocks, rows, cols, perm, plan)
    copies[3].wait()
    for h in range(HEADB):
        head_x[h] = x[perm[0, 0, h]]
    core = lax.axis_index("level") & 1
    for j in range(blocks // 2):
        mine[j] = x[core * (blocks // 2) + j]
    copies[4].wait()
    target = lambda s, t, piece: t
    for_tiles(count, plan, vals, HEAD_ROW, [(lambda v, s, t: dot(v, x[s]), target)], acc, 2 * HEADB)
    for_tiles(count, plan, vals, HEAD_COL, [(lambda v, s, t: dot_t(v, x[s]), target)], acc, 2 * HEADB)
    for i in range(2 * HEADB):
        plain[i] = acc[i]
        put_coded(coded, i, acc[i])


def receives(step):
    return lax.axis_index("band") % (2 * step) == step


def heads_add_kernel(step, had, came, head_x, head_got, coded, plain, head_out):
    for i in range(had.shape[0]):
        value = had[i] + get_coded(came, i)
        plain[i] = value
        put_coded(coded, i, value)
    head_out[...] = jnp.where(receives(step), head_got[...], head_x[...])


def halo_out_kernel(count, blocks, shares, x, vals, plan, near, send, keep, acc, table):
    acc[...] = jnp.zeros_like(acc)
    for part, side in enumerate(sides(lax.axis_index("band"))):
        for j in range(blocks):
            for piece in range(shares.pieces):
                table[(part * 2 * blocks + j) * shares.pieces + piece] = shares.slot(
                    part, near[side * blocks + j], piece
                )
    near_slot = lambda s, t, piece: table[t * shares.pieces + piece]
    for_tiles(count, plan, vals, NEAR, [(lambda v, s, t: dot_t(v, x[s]), near_slot)], acc, shares.slots)
    half = shares.slots // 2
    send[...] = acc[:half].reshape(send.shape)
    keep[...] = acc[half : 2 * half].reshape(keep.shape)


def own_kernel(count, shares, x, vals, plan, own, acc):
    acc[...] = jnp.zeros_like(acc)
    forward = (lambda v, s, t: dot(v, x[t]), lambda s, t, piece: shares.slot(0, s, piece))
    backward = (lambda v, s, t: dot_t(v, x[s]), lambda s, t, piece: shares.slot(1, t, piece))
    for_tiles(count, plan, vals, OWN, [forward, backward], acc, shares.slots)
    own[...] = acc[: shares.slots]


def remote_kernel(count, blocks, shares, vals, plan, near, own, pair, pair2, other, other2, head_x, head_got, send, keep, acc, xw, table):
    half_blocks = blocks // 2
    core = lax.axis_index("level") & 1
    for j in range(half_blocks):
        for at, (mine, swapped) in enumerate(((pair, pair2), (other, other2))):
            xw[at * blocks + core * half_blocks + j] = mine[j]
            xw[at * blocks + (1 - core) * half_blocks + j] = swapped[j]
    for j in range(HEADB):
        xw[2 * blocks + j] = jnp.where(receives(1), head_got[j], head_x[j])
        table[3 * blocks + j] = 2 * blocks + j
    for part, side in enumerate(sides(lax.axis_index("band"))):
        for j in range(blocks):
            table[part * 2 * blocks + j] = side * blocks + near[side * blocks + j]
    acc[: shares.slots] = own[...]
    forward = (lambda v, s, t: dot(v, xw[table[s]]), lambda s, t, piece: shares.slot(0, t, piece))
    backward = (lambda v, s, t: dot_t(v, xw[2 * blocks + t]), lambda s, t, piece: shares.slot(1, s, piece))
    for_tiles(count, plan, vals, REMOTE, [forward], acc, shares.slots)
    for_tiles(count, plan, vals, HEAD_ROW, [backward], acc, shares.slots)
    half = shares.slots // 2
    send[...] = acc[:half].reshape(send.shape)
    keep[...] = acc[half : 2 * half].reshape(keep.shape)


def heads_in_kernel(shares, perm, send_in, keep_in, had, came, send, keep):
    send[...] = send_in[...]
    keep[...] = keep_in[...]

    @pl.when(lax.axis_index("band") == 0)
    def _():
        half = shares.slots // 2
        for part in range(2):
            for h in range(HEADB):
                value = had[part * HEADB + h] + get_coded(came, part * HEADB + h)
                for piece in range(shares.pieces):
                    slot = shares.slot(part, perm[h], piece)
                    some = value[piece * shares.unit : (piece + 1) * shares.unit]

                    @pl.when(slot < half)
                    def _():
                        send[slot] += some

                    @pl.when(slot >= half)
                    def _():
                        keep[slot - half] += some


def split_kernel(bit, coded_in, had, came, send, keep):
    mine = (lax.axis_index("level") >> bit) & 1
    parts, m, share, width = had.shape
    for part in range(parts):
        for i in range(m // 2):
            for half in range(2):
                j = 2 * i + (mine if half else 1 - mine)
                came_value = get_coded(came, part * m + j) if coded_in else came[part, j]
                value = had[part, j] + came_value
                if half:
                    keep[part, i] = value
                else:
                    put_coded(send, part * (m // 2) + i, value)


def edge_kernel(coded_in, had, came, relayed, direct):
    odd = lax.axis_index("band") & 1
    for side, part in ((0, 1 - odd), (1, odd)):
        came_value = get_coded(came, part) if coded_in else came[part, 0]
        value = had[part, 0] + came_value
        if side:
            put_coded(relayed, 0, value)
        else:
            direct[0] = value


def relay_kernel(direct, came, out):
    put_coded(out, 0, direct[0] + get_coded(came, 0))


def last_kernel(coded_in, had, came, from_near, forward, backward):
    came_values = [get_coded(came, part) if coded_in else came[part, 0] for part in range(2)]
    forward[0] = (had[0, 0] + came_values[0]).astype(forward.dtype)
    backward[0] = (had[1, 0] + came_values[1] + get_coded(from_near, 0)).astype(backward.dtype)


def over_levels(send, keep, levels, after=()):
    bit, coded = 0, False
    parts, m, share, width = keep.shape
    while True:
        pairs = [(i, i ^ (1 << bit)) for i in range(levels)]
        came = lax.ppermute(send, "level", pairs)
        if m == 1:
            return keep, came, coded
        bit += 1
        send, keep = call(
            functools.partial(split_kernel, bit, coded),
            (array((parts * (m // 2), share + GROUPS, width), I16), array((parts, m // 2, share, width))),
            (keep, came),
            after=after,
        )
        coded = True
        m //= 2


def on_device(features, block_perm, tile_rows, tile_cols, tile_vals):
    rdev, width = features.shape
    blocks = block_perm.shape[2]
    tile = tile_vals.shape[2]
    count = tile_vals.shape[1]
    levels = lax.axis_size("level")
    bands = lax.axis_size("band")
    band = lax.axis_index("band")
    cores = [(i, i ^ 1) for i in range(levels)]
    pairs = [(i, i ^ 1) for i in range(bands)]
    outward = [(i, i + 2 if i % 2 else i - 2) for i in range(bands)]
    outward = [(i, j) for i, j in outward if 0 <= j < bands]
    inward = [(j, i) for i, j in outward]
    shares = Shares(levels, rdev, tile, 2)
    share, m, unit = shares.share, shares.m, shares.unit

    perm = block_perm[0, 0]
    vals = tile_vals[0]
    x = features.reshape(blocks, tile, width)
    pair_perm = lax.ppermute(perm, "band", pairs)
    other_perm = lax.ppermute(pair_perm, "band", inward)
    near = jnp.concatenate([pair_perm, other_perm])

    coded_heads = array((2 * HEADB, tile + GROUPS, width), I16)
    plain_heads = array((2 * HEADB, tile, width))
    in_hbm = lambda a: pltpu.with_memory_space_constraint(a, pltpu.HBM)
    plan, coded, heads, xh, mine, x, vals = call(
        functools.partial(heads_out_kernel, count, blocks),
        (
            array((5 * count + 5,), jnp.int32),
            coded_heads,
            plain_heads,
            array((HEADB, tile, width), x.dtype),
            array((blocks // 2, tile, width), x.dtype),
            pltpu.VMEM(x.shape, x.dtype),
            pltpu.VMEM(vals.shape, vals.dtype),
        ),
        tuple(in_hbm(a) for a in (tile_rows, tile_cols, block_perm, x, vals)),
        (
            pltpu.VMEM((2 * HEADB + 1, tile, width), F32),
            pltpu.SMEM(tile_rows.shape, jnp.int32),
            pltpu.SMEM(tile_cols.shape, jnp.int32),
            pltpu.SMEM(block_perm.shape, jnp.int32),
            pltpu.SemaphoreType.DMA((5,)),
        ),
        in_hbm=5,
        after=(pair_perm,),
    )
    x, vals = (pltpu.with_memory_space_constraint(a, pltpu.VMEM) for a in (x, vals))

    pair_x = lax.ppermute(mine, "band", pairs)
    other_x = lax.ppermute(pair_x, "band", inward)
    pair_x2 = lax.ppermute(pair_x, "level", cores)
    other_x2 = lax.ppermute(other_x, "level", cores)

    half_shape = array((2, m, share, width))
    halo_out = functools.partial(
        call,
        functools.partial(halo_out_kernel, count, blocks, shares),
        (half_shape, half_shape),
        (x, vals, plan, near),
        (
            pltpu.VMEM((shares.slots + 1, unit, width), F32),
            pltpu.SMEM((3 * blocks * shares.pieces,), jnp.int32),
        ),
    )
    own = call(
        functools.partial(own_kernel, count, shares),
        (array((shares.slots, unit, width)),),
        (x, vals, plan),
        (pltpu.VMEM((shares.slots + 1, unit, width), F32),),
    )[0]

    order = [1 << i for i in range(1, bands.bit_length() - 1)] + [1]
    fences = [(near, pair_x), (other_x,)] + [()] * bands
    done = 0
    for at, bit in enumerate(order):
        step = bands >> (at + 1)
        senders = [i for i in range(bands) if i & bit and not i & done]
        done |= bit
        came = lax.ppermute(coded, "band", [(i, i - bit) for i in senders])
        got = lax.ppermute(xh, "band", [(i, i + step) for i in range(0, bands, 2 * step)])
        if at == 1:
            halo_send, halo_keep = halo_out(after=(coded,))
            halo = over_levels(halo_send, halo_keep, levels)
            fences[1] += (halo_send, own)
        if bit != order[-1]:
            coded, heads, xh = call(
                functools.partial(heads_add_kernel, step),
                (coded_heads, plain_heads, array(xh.shape, xh.dtype)),
                (heads, came, xh, got),
                after=fences[at],
            )

    halo_had, halo_came, halo_coded = halo
    relayed, direct = call(
        functools.partial(edge_kernel, halo_coded),
        (array((1, share + GROUPS, width), I16), array((1, share, width))),
        (halo_had, halo_came),
    )
    relayed = lax.ppermute(relayed, "band", outward)
    to_pair = call(relay_kernel, (array((1, share + GROUPS, width), I16),), (direct, relayed))[0]
    from_near = lax.ppermute(to_pair, "band", pairs)

    send, keep = call(
        functools.partial(remote_kernel, count, blocks, shares),
        (half_shape, half_shape),
        (vals, plan, near, own, pair_x, pair_x2, other_x, other_x2, xh, got),
        (
            pltpu.VMEM((shares.slots + 1, unit, width), F32),
            pltpu.VMEM((2 * blocks + HEADB, tile, width), features.dtype),
            pltpu.SMEM((3 * blocks + HEADB,), jnp.int32),
        ),
        after=(relayed,),
    )
    flat = array((shares.slots // 2, unit, width))
    send, keep = call(
        functools.partial(heads_in_kernel, shares),
        (flat, flat),
        (perm, send.reshape(flat.shape), keep.reshape(flat.shape), heads, came),
        after=(to_pair,),
    )
    had, came, was_coded = over_levels(send.reshape(half_shape.shape), keep.reshape(half_shape.shape), levels)
    out = array((1, share, width), jnp.bfloat16)
    forward, backward = call(functools.partial(last_kernel, was_coded), (out, out), (had, came, from_near))
    return forward, backward


def solution(mesh):
    return jax.shard_map(
        on_device,
        mesh=mesh,
        in_specs=(
            P("band", None),
            P("level", "band", None),
            P("level", "band"),
            P("level", "band"),
            P("level", "band", None, None),
        ),
        out_specs=(P("band", "level", None), P("band", "level", None)),
        check_vma=False,
    )
```

```python
import functools
import math

import jax
import jax.numpy as jnp
from jax import lax
from jax.experimental import pallas as pl
from jax.experimental.pallas import tpu as pltpu
from jax.sharding import PartitionSpec as P

HEADB = 2
GROUPS = 16
UNROLL = 4
PAD_ROWS = 128
VMEM_LIMIT = 24 * 2**20
F32 = jnp.float32
I16 = jnp.int16
VMEM = pl.BlockSpec(memory_space=pltpu.VMEM)
ANY = pl.BlockSpec(memory_space=pl.ANY)
HBM = pl.BlockSpec(memory_space=pltpu.HBM)
SMEM = pl.BlockSpec(memory_space=pltpu.SMEM)


def call(kernel, outs, ins, scratch=(), after=(), in_hbm=0, through=()):
    bytes_moved = sum(math.prod(a.shape) * a.dtype.itemsize for a in (*outs, *ins))

    def body(*refs):
        outputs = len(ins) + len(after) + len(through)
        kernel(*refs[: len(ins)], *refs[outputs : outputs + len(outs)], *refs[outputs + len(outs) + len(through) :])

    return pl.pallas_call(
        body,
        out_shape=[*outs, *(array(a.shape, a.dtype) for a in through)],
        in_specs=[HBM] * in_hbm + [SMEM if a.ndim == 1 else VMEM for a in ins[in_hbm:]] + [ANY] * len((*after, *through)),
        out_specs=[SMEM if len(a.shape) == 1 else VMEM for a in outs] + [ANY] * len(through),
        input_output_aliases={len(ins) + len(after) + i: len(outs) + i for i in range(len(through))},
        scratch_shapes=list(scratch),
        compiler_params=pltpu.CompilerParams(vmem_limit_bytes=VMEM_LIMIT),
        cost_estimate=pl.CostEstimate(flops=0, bytes_accessed=bytes_moved, transcendentals=0),
    )(*ins, *after, *through)


def array(shape, dtype=F32):
    return jax.ShapeDtypeStruct(tuple(shape), dtype)


def encode(value):
    rows, width = value.shape
    grouped = value.reshape(GROUPS, rows // GROUPS, width)
    largest = jnp.maximum(jnp.max(jnp.abs(grouped), axis=1), 1e-30)
    power = jnp.ceil(jnp.log2(largest))
    scaled = jnp.round(grouped * jnp.exp2(15.0 - power)[:, None, :])
    codes = jnp.clip(scaled, -32767.0, 32767.0).astype(jnp.int32).astype(I16)
    return codes.reshape(rows, width), power.astype(jnp.int32).astype(I16)


def put_coded(ref, index, value):
    rows = value.shape[0]
    codes, power = encode(value)
    ref[index, :rows, :] = codes
    ref[index, rows:, :] = power


def get_coded(ref, index):
    rows, width = ref.shape[-2] - GROUPS, ref.shape[-1]
    codes = ref[index, :rows, :].astype(jnp.int32).astype(F32)
    power = ref[index, rows:, :].astype(jnp.int32).astype(F32)
    grouped = codes.reshape(GROUPS, rows // GROUPS, width) * jnp.exp2(power - 15.0)[:, None, :]
    return grouped.reshape(rows, width)


def dot(a, b):
    return jnp.dot(a, b, preferred_element_type=F32)


def dot_t(a, b):
    return lax.dot_general(a, b, (((0,), (0,)), ((), ())), preferred_element_type=F32)


HEAD_ROW, HEAD_COL, NEAR, OWN, REMOTE = range(5)


def packed(k, source, target):
    return k | (source << 8) | (target << 16)


def write_plan(count, blocks, rows, cols, perm, plan):
    low = lax.axis_index("band") * blocks
    n = [jnp.int32(0)] * 5
    for k in range(count):
        row, col = rows[0, k] - low, cols[0, k] - low
        own_row = (row >= 0) & (row < blocks)
        own_col = (col >= 0) & (col < blocks)
        near = (col >= -blocks) & (col < 2 * blocks)
        x_row = perm[0, 0, jnp.clip(row, 0, blocks - 1)]
        x_col = perm[0, 0, jnp.clip(col, 0, blocks - 1)]
        near_at = jnp.where(near, col + blocks, 3 * blocks + cols[0, k])
        for which, chosen, source, target in (
            (HEAD_ROW, ~own_row, x_col, rows[0, k]),
            (HEAD_COL, own_row & ~near, x_row, HEADB + cols[0, k]),
            (NEAR, own_row & near & ~own_col, x_row, near_at),
            (OWN, own_row & own_col, x_row, x_col),
            (REMOTE, own_row & ~own_col, near_at, x_row),
        ):
            plan[which * count + n[which]] = packed(k, source, target)
            n[which] = n[which] + chosen.astype(jnp.int32)
    for which in range(5):
        plan[5 * count + which] = n[which]


def for_tiles(count, plan, vals, which, jobs, acc, trash):
    n = plan[5 * count + which]
    unit = acc.shape[1]

    def step(i, carry):
        entries = []
        for u in range(UNROLL):
            real = i * UNROLL + u < n
            e = plan[which * count + jnp.minimum(i * UNROLL + u, n - 1)]
            entries.append((real, e & 255, (e >> 8) & 255, e >> 16))
        products = [[product(vals[k], s, t) for product, _ in jobs] for _, k, s, t in entries]
        for values, (real, _, s, t) in zip(products, entries):
            for value, (_, place) in zip(values, jobs):
                for piece in range(value.shape[0] // unit):
                    slot = jnp.where(real, place(s, t, piece), trash)
                    acc[slot] += value[piece * unit : (piece + 1) * unit]
        return carry

    lax.fori_loop(0, (n + UNROLL - 1) // UNROLL, step, 0)


class Shares:
    def __init__(self, levels, rdev, tile, parts):
        self.share = rdev // levels
        self.unit = min(tile, self.share)
        self.per = self.share // self.unit
        self.m = levels // 2
        self.parts = parts
        self.tile = tile
        self.pieces = tile // self.unit
        self.slots = 2 * parts * self.m * self.per

    def slot(self, part, block, piece):
        at = block * self.pieces + piece
        owner = at // self.per
        keep = 1 - ((owner ^ lax.axis_index("level")) & 1)
        return ((keep * self.parts + part) * self.m + (owner >> 1)) * self.per + at % self.per


def sides(band):
    odd = band & 1
    return 1 - odd, odd


def heads_out_kernel(count, blocks, rows_hbm, cols_hbm, perm_hbm, x_hbm, vals_hbm, plan, coded, plain, head_x, x, vals, acc, rows, cols, perm, few):
    copies = [
        pltpu.make_async_copy(a, b, few.at[i])
        for i, (a, b) in enumerate(((rows_hbm, rows), (cols_hbm, cols), (perm_hbm, perm), (x_hbm, x), (vals_hbm, vals)))
    ]
    for copy in copies:
        copy.start()
    acc[...] = jnp.zeros_like(acc)
    for copy in copies[:3]:
        copy.wait()
    write_plan(count, blocks, rows, cols, perm, plan)
    copies[3].wait()
    for h in range(HEADB):
        head_x[h] = x[perm[0, 0, h]]
    copies[4].wait()
    target = lambda s, t, piece: t
    for_tiles(count, plan, vals, HEAD_ROW, [(lambda v, s, t: dot(v, x[s]), target)], acc, 2 * HEADB)
    for_tiles(count, plan, vals, HEAD_COL, [(lambda v, s, t: dot_t(v, x[s]), target)], acc, 2 * HEADB)
    for i in range(2 * HEADB):
        plain[i] = acc[i]
        put_coded(coded, i, acc[i])


def heads_take_kernel(step, head_x, head_got, out):
    out[...] = jnp.where(lax.axis_index("band") % (2 * step) == step, head_got[...], head_x[...])


def heads_add_kernel(had, came, coded, plain):
    for i in range(had.shape[0]):
        value = had[i] + get_coded(came, i)
        plain[i] = value
        put_coded(coded, i, value)


def halo_out_kernel(count, blocks, shares, x, vals, plan, near, send, keep, acc, table):
    acc[...] = jnp.zeros_like(acc)
    for part, side in enumerate(sides(lax.axis_index("band"))):
        for j in range(blocks):
            for piece in range(shares.pieces):
                table[(part * 2 * blocks + j) * shares.pieces + piece] = shares.slot(
                    part, near[side * blocks + j], piece
                )
    near_slot = lambda s, t, piece: table[t * shares.pieces + piece]
    for_tiles(count, plan, vals, NEAR, [(lambda v, s, t: dot_t(v, x[s]), near_slot)], acc, shares.slots)
    half = shares.slots // 2
    send[...] = acc[:half].reshape(send.shape)
    keep[...] = acc[half : 2 * half].reshape(keep.shape)


def own_kernel(count, shares, x, vals, plan, own, acc):
    acc[...] = jnp.zeros_like(acc)
    forward = (lambda v, s, t: dot(v, x[t]), lambda s, t, piece: shares.slot(0, s, piece))
    backward = (lambda v, s, t: dot_t(v, x[s]), lambda s, t, piece: shares.slot(1, t, piece))
    for_tiles(count, plan, vals, OWN, [forward, backward], acc, shares.slots)
    own[...] = acc[: shares.slots]


def remote_kernel(count, blocks, shares, vals, plan, near, own, pair, pair2, other, other2, head_x, send, keep, acc, xw, table):
    half_blocks = blocks // 2
    tile = xw.shape[1]
    core = lax.axis_index("level") & 1
    for j in range(half_blocks):
        for at, (mine, swapped) in enumerate(((pair, pair2), (other, other2))):
            xw[at * blocks + core * half_blocks + j] = mine[j * tile : (j + 1) * tile]
            xw[at * blocks + (1 - core) * half_blocks + j] = swapped[j * tile : (j + 1) * tile]
    for j in range(HEADB):
        xw[2 * blocks + j] = head_x[j]
        table[3 * blocks + j] = 2 * blocks + j
    for part, side in enumerate(sides(lax.axis_index("band"))):
        for j in range(blocks):
            table[part * 2 * blocks + j] = side * blocks + near[side * blocks + j]
    acc[: shares.slots] = own[...]
    forward = (lambda v, s, t: dot(v, xw[table[s]]), lambda s, t, piece: shares.slot(0, t, piece))
    backward = (lambda v, s, t: dot_t(v, xw[2 * blocks + t]), lambda s, t, piece: shares.slot(1, s, piece))
    for_tiles(count, plan, vals, REMOTE, [forward], acc, shares.slots)
    for_tiles(count, plan, vals, HEAD_ROW, [backward], acc, shares.slots)
    half = shares.slots // 2
    send[...] = acc[:half].reshape(send.shape)
    keep[...] = acc[half : 2 * half].reshape(keep.shape)


def heads_in_kernel(shares, perm, send_in, keep_in, had, came, send, keep):
    send[...] = send_in[...]
    keep[...] = keep_in[...]

    @pl.when(lax.axis_index("band") == 0)
    def _():
        half = shares.slots // 2
        for part in range(2):
            for h in range(HEADB):
                value = had[part * HEADB + h] + get_coded(came, part * HEADB + h)
                for piece in range(shares.pieces):
                    slot = shares.slot(part, perm[h], piece)
                    some = value[piece * shares.unit : (piece + 1) * shares.unit]

                    @pl.when(slot < half)
                    def _():
                        send[slot] += some

                    @pl.when(slot >= half)
                    def _():
                        keep[slot - half] += some


def split_kernel(bit, coded_in, had, came, send, keep):
    mine = (lax.axis_index("level") >> bit) & 1
    parts, m, share, width = had.shape
    for part in range(parts):
        for i in range(m // 2):
            for half in range(2):
                j = 2 * i + (mine if half else 1 - mine)
                came_value = get_coded(came, part * m + j) if coded_in else came[part, j]
                value = had[part, j] + came_value
                if half:
                    keep[part, i] = value
                else:
                    put_coded(send, part * (m // 2) + i, value)


def edge_kernel(coded_in, had, came, relayed, direct):
    odd = lax.axis_index("band") & 1
    for side, part in ((0, 1 - odd), (1, odd)):
        came_value = get_coded(came, part) if coded_in else came[part, 0]
        value = had[part, 0] + came_value
        if side:
            put_coded(relayed, 0, value)
        else:
            direct[0] = value


def relay_kernel(direct, came, out):
    put_coded(out, 0, direct[0] + get_coded(came, 0))


def last_kernel(coded_in, had, came, from_near, forward, backward):
    came_values = [get_coded(came, part) if coded_in else came[part, 0] for part in range(2)]
    forward[0] = (had[0, 0] + came_values[0]).astype(forward.dtype)
    backward[0] = (had[1, 0] + came_values[1] + get_coded(from_near, 0)).astype(backward.dtype)


def over_levels(send, keep, levels, after=()):
    bit, coded = 0, False
    parts, m, share, width = keep.shape
    while True:
        pairs = [(i, i ^ (1 << bit)) for i in range(levels)]
        came = lax.ppermute(send, "level", pairs)
        if m == 1:
            return keep, came, coded
        bit += 1
        send, keep = call(
            functools.partial(split_kernel, bit, coded),
            (array((parts * (m // 2), share + GROUPS, width), I16), array((parts, m // 2, share, width))),
            (keep, came),
            after=after,
        )
        coded = True
        m //= 2


def on_device(features, block_perm, tile_rows, tile_cols, tile_vals):
    rdev, width = features.shape
    blocks = block_perm.shape[2]
    tile = tile_vals.shape[2]
    count = tile_vals.shape[1]
    levels = lax.axis_size("level")
    bands = lax.axis_size("band")
    band = lax.axis_index("band")
    cores = [(i, i ^ 1) for i in range(levels)]
    pairs = [(i, i ^ 1) for i in range(bands)]
    outward = [(i, i + 2 if i % 2 else i - 2) for i in range(bands)]
    outward = [(i, j) for i, j in outward if 0 <= j < bands]
    inward = [(j, i) for i, j in outward]
    shares = Shares(levels, rdev, tile, 2)
    share, m, unit = shares.share, shares.m, shares.unit

    perm = block_perm[0, 0]
    vals = tile_vals[0]
    x = features.reshape(blocks, tile, width)
    half = lax.dynamic_slice_in_dim(features, (lax.axis_index("level") & 1) * (rdev // 2), rdev // 2, 0)
    order_row = jnp.pad(perm.astype(features.dtype)[None], ((0, PAD_ROWS - 1), (0, width - blocks)))
    mine = jnp.concatenate([half, order_row])
    pair_x = lax.ppermute(mine, "band", pairs)
    other_x = lax.ppermute(pair_x, "band", inward)
    pair_x2 = lax.ppermute(pair_x, "level", cores)
    other_x2 = lax.ppermute(other_x, "level", cores)
    near = jnp.concatenate([a[rdev // 2, :blocks] for a in (pair_x, other_x)]).astype(jnp.int32)

    coded_heads = array((2 * HEADB, tile + GROUPS, width), I16)
    plain_heads = array((2 * HEADB, tile, width))
    in_hbm = lambda a: pltpu.with_memory_space_constraint(a, pltpu.HBM)
    plan, coded, heads, xh, x, vals = call(
        functools.partial(heads_out_kernel, count, blocks),
        (
            array((5 * count + 5,), jnp.int32),
            coded_heads,
            plain_heads,
            array((HEADB, tile, width), x.dtype),
            pltpu.VMEM(x.shape, x.dtype),
            pltpu.VMEM(vals.shape, vals.dtype),
        ),
        tuple(in_hbm(a) for a in (tile_rows, tile_cols, block_perm, x, vals)),
        (
            pltpu.VMEM((2 * HEADB + 1, tile, width), F32),
            pltpu.SMEM(tile_rows.shape, jnp.int32),
            pltpu.SMEM(tile_cols.shape, jnp.int32),
            pltpu.SMEM(block_perm.shape, jnp.int32),
            pltpu.SemaphoreType.DMA((5,)),
        ),
        in_hbm=5,
    )
    x, vals = (pltpu.with_memory_space_constraint(a, pltpu.VMEM) for a in (x, vals))

    half_shape = array((2, m, share, width))
    halo_out = functools.partial(
        call,
        functools.partial(halo_out_kernel, count, blocks, shares),
        (half_shape, half_shape),
        (x, vals, plan, near),
        (
            pltpu.VMEM((shares.slots + 1, unit, width), F32),
            pltpu.SMEM((3 * blocks * shares.pieces,), jnp.int32),
        ),
    )
    own = call(
        functools.partial(own_kernel, count, shares),
        (array((shares.slots, unit, width)),),
        (x, vals, plan),
        (pltpu.VMEM((shares.slots + 1, unit, width), F32),),
    )[0]

    order = [1 << i for i in range(1, bands.bit_length() - 1)] + [1]
    halo_send = halo_keep = None
    fences = [(pair_x,), (own,)] + [()] * bands
    done = 0
    for at, bit in enumerate(order):
        step = bands >> (at + 1)
        senders = [i for i in range(bands) if i & bit and not i & done]
        done |= bit
        came = lax.ppermute(coded, "band", [(i, i - bit) for i in senders])
        got = lax.ppermute(xh, "band", [(i, i + step) for i in range(0, bands, 2 * step)])
        if at == 1:
            halo_send, halo_keep = halo_out(after=(coded, got))
        if bit != order[-1]:
            coded, heads, *passed = call(
                heads_add_kernel,
                (coded_heads, plain_heads),
                (heads, came),
                after=fences[at],
                through=(halo_send,) if at == 1 else (),
            )
            halo_send = passed[0] if passed else halo_send
        xh = call(
            functools.partial(heads_take_kernel, step), (array(xh.shape, xh.dtype),), (xh, got), after=(coded,)
        )[0]
    halo_had, halo_came, halo_coded = over_levels(halo_send, halo_keep, levels)

    send, keep = call(
        functools.partial(remote_kernel, count, blocks, shares),
        (half_shape, half_shape),
        (vals, plan, near, own, pair_x, pair_x2, other_x, other_x2, xh),
        (
            pltpu.VMEM((shares.slots + 1, unit, width), F32),
            pltpu.VMEM((2 * blocks + HEADB, tile, width), features.dtype),
            pltpu.SMEM((3 * blocks + HEADB,), jnp.int32),
        ),
        after=(halo_had,),
    )
    flat = array((shares.slots // 2, unit, width))
    send, keep = call(
        functools.partial(heads_in_kernel, shares),
        (flat, flat),
        (perm, send.reshape(flat.shape), keep.reshape(flat.shape), heads, came),
        after=(halo_came,),
    )
    relayed, direct = call(
        functools.partial(edge_kernel, halo_coded),
        (array((1, share + GROUPS, width), I16), array((1, share, width))),
        (halo_had, halo_came),
    )
    had, came, was_coded = over_levels(send.reshape(half_shape.shape), keep.reshape(half_shape.shape), levels, after=(direct,))
    relayed = lax.ppermute(relayed, "band", outward)
    to_pair = call(relay_kernel, (array((1, share + GROUPS, width), I16),), (direct, relayed))[0]
    from_near = lax.ppermute(to_pair, "band", pairs)

    out = array((1, share, width), jnp.bfloat16)
    forward, backward = call(functools.partial(last_kernel, was_coded), (out, out), (had, came, from_near))
    return forward, backward


def solution(mesh):
    return jax.shard_map(
        on_device,
        mesh=mesh,
        in_specs=(
            P("band", None),
            P("level", "band", None),
            P("level", "band"),
            P("level", "band"),
            P("level", "band", None, None),
        ),
        out_specs=(P("band", "level", None), P("band", "level", None)),
        check_vma=False,
    )
```

```python
import functools
import math

import jax
import jax.numpy as jnp
from jax import lax
from jax.experimental import pallas as pl
from jax.experimental.pallas import tpu as pltpu
from jax.sharding import PartitionSpec as P

HEADB = 2
GROUPS = 16
UNROLL = 4
PAD_ROWS = 128
VMEM_LIMIT = 24 * 2**20
F32 = jnp.float32
I16 = jnp.int16
VMEM = pl.BlockSpec(memory_space=pltpu.VMEM)
ANY = pl.BlockSpec(memory_space=pl.ANY)
HBM = pl.BlockSpec(memory_space=pltpu.HBM)
SMEM = pl.BlockSpec(memory_space=pltpu.SMEM)


def call(kernel, outs, ins, scratch=(), after=(), in_hbm=0, through=()):
    bytes_moved = sum(math.prod(a.shape) * a.dtype.itemsize for a in (*outs, *ins))

    def body(*refs):
        outputs = len(ins) + len(after) + len(through)
        kernel(*refs[: len(ins)], *refs[outputs : outputs + len(outs)], *refs[outputs + len(outs) + len(through) :])

    return pl.pallas_call(
        body,
        out_shape=[*outs, *(array(a.shape, a.dtype) for a in through)],
        in_specs=[HBM] * in_hbm + [SMEM if a.ndim == 1 else VMEM for a in ins[in_hbm:]] + [ANY] * len((*after, *through)),
        out_specs=[SMEM if len(a.shape) == 1 else VMEM for a in outs] + [ANY] * len(through),
        input_output_aliases={len(ins) + len(after) + i: len(outs) + i for i in range(len(through))},
        scratch_shapes=list(scratch),
        compiler_params=pltpu.CompilerParams(vmem_limit_bytes=VMEM_LIMIT),
        cost_estimate=pl.CostEstimate(flops=0, bytes_accessed=bytes_moved, transcendentals=0),
    )(*ins, *after, *through)


def array(shape, dtype=F32):
    return jax.ShapeDtypeStruct(tuple(shape), dtype)


def encode(value):
    rows, width = value.shape
    grouped = value.reshape(GROUPS, rows // GROUPS, width)
    largest = jnp.maximum(jnp.max(jnp.abs(grouped), axis=1), 1e-30)
    power = jnp.ceil(jnp.log2(largest))
    scaled = jnp.round(grouped * jnp.exp2(15.0 - power)[:, None, :])
    codes = jnp.clip(scaled, -32767.0, 32767.0).astype(jnp.int32).astype(I16)
    return codes.reshape(rows, width), power.astype(jnp.int32).astype(I16)


def put_coded(ref, index, value):
    rows = value.shape[0]
    codes, power = encode(value)
    ref[index, :rows, :] = codes
    ref[index, rows:, :] = power


def get_coded(ref, index):
    rows, width = ref.shape[-2] - GROUPS, ref.shape[-1]
    codes = ref[index, :rows, :].astype(jnp.int32).astype(F32)
    power = ref[index, rows:, :].astype(jnp.int32).astype(F32)
    grouped = codes.reshape(GROUPS, rows // GROUPS, width) * jnp.exp2(power - 15.0)[:, None, :]
    return grouped.reshape(rows, width)


def dot(a, b):
    return jnp.dot(a, b, preferred_element_type=F32)


def dot_t(a, b):
    return lax.dot_general(a, b, (((0,), (0,)), ((), ())), preferred_element_type=F32)


HEAD_ROW, HEAD_COL, NEAR, OWN, REMOTE = range(5)


def packed(k, source, target):
    return k | (source << 8) | (target << 16)


def write_plan(count, blocks, rows, cols, perm, plan):
    low = lax.axis_index("band") * blocks
    n = [jnp.int32(0)] * 5
    for k in range(count):
        row, col = rows[0, k] - low, cols[0, k] - low
        own_row = (row >= 0) & (row < blocks)
        own_col = (col >= 0) & (col < blocks)
        near = (col >= -blocks) & (col < 2 * blocks)
        x_row = perm[0, 0, jnp.clip(row, 0, blocks - 1)]
        x_col = perm[0, 0, jnp.clip(col, 0, blocks - 1)]
        near_at = jnp.where(near, col + blocks, 3 * blocks + cols[0, k])
        for which, chosen, source, target in (
            (HEAD_ROW, ~own_row, x_col, rows[0, k]),
            (HEAD_COL, own_row & ~near, x_row, HEADB + cols[0, k]),
            (NEAR, own_row & near & ~own_col, x_row, near_at),
            (OWN, own_row & own_col, x_row, x_col),
            (REMOTE, own_row & ~own_col, near_at, x_row),
        ):
            plan[which * count + n[which]] = packed(k, source, target)
            n[which] = n[which] + chosen.astype(jnp.int32)
    for which in range(5):
        plan[5 * count + which] = n[which]


def for_tiles(count, plan, vals, which, jobs, acc, trash):
    n = plan[5 * count + which]
    unit = acc.shape[1]

    def step(i, carry):
        entries = []
        for u in range(UNROLL):
            real = i * UNROLL + u < n
            e = plan[which * count + jnp.minimum(i * UNROLL + u, n - 1)]
            entries.append((real, e & 255, (e >> 8) & 255, e >> 16))
        products = [[product(vals[k], s, t) for product, _ in jobs] for _, k, s, t in entries]
        for values, (real, _, s, t) in zip(products, entries):
            for value, (_, place) in zip(values, jobs):
                for piece in range(value.shape[0] // unit):
                    slot = jnp.where(real, place(s, t, piece), trash)
                    acc[slot] += value[piece * unit : (piece + 1) * unit]
        return carry

    lax.fori_loop(0, (n + UNROLL - 1) // UNROLL, step, 0)


class Shares:
    def __init__(self, levels, rdev, tile, parts):
        self.share = rdev // levels
        self.unit = min(tile, self.share)
        self.per = self.share // self.unit
        self.m = levels // 2
        self.parts = parts
        self.tile = tile
        self.pieces = tile // self.unit
        self.slots = 2 * parts * self.m * self.per

    def slot(self, part, block, piece):
        at = block * self.pieces + piece
        owner = at // self.per
        keep = 1 - ((owner ^ lax.axis_index("level")) & 1)
        return ((keep * self.parts + part) * self.m + (owner >> 1)) * self.per + at % self.per


def sides(band):
    odd = band & 1
    return 1 - odd, odd


def heads_out_kernel(count, blocks, rows_hbm, cols_hbm, perm_hbm, x_hbm, vals_hbm, plan, coded, plain, head_x, x, vals, acc, rows, cols, perm, few):
    copies = [
        pltpu.make_async_copy(a, b, few.at[i])
        for i, (a, b) in enumerate(((rows_hbm, rows), (cols_hbm, cols), (perm_hbm, perm), (x_hbm, x), (vals_hbm, vals)))
    ]
    for copy in copies:
        copy.start()
    acc[...] = jnp.zeros_like(acc)
    for copy in copies[:3]:
        copy.wait()
    write_plan(count, blocks, rows, cols, perm, plan)
    copies[3].wait()
    for h in range(HEADB):
        head_x[h] = x[perm[0, 0, h]]
    copies[4].wait()
    target = lambda s, t, piece: t
    for_tiles(count, plan, vals, HEAD_ROW, [(lambda v, s, t: dot(v, x[s]), target)], acc, 2 * HEADB)
    for_tiles(count, plan, vals, HEAD_COL, [(lambda v, s, t: dot_t(v, x[s]), target)], acc, 2 * HEADB)
    for i in range(2 * HEADB):
        plain[i] = acc[i]
        put_coded(coded, i, acc[i])


def heads_take_kernel(step, head_x, head_got, out):
    out[...] = jnp.where(lax.axis_index("band") % (2 * step) == step, head_got[...], head_x[...])


def heads_add_kernel(had, came, coded, plain):
    for i in range(had.shape[0]):
        value = had[i] + get_coded(came, i)
        plain[i] = value
        put_coded(coded, i, value)


def halo_out_kernel(count, blocks, shares, x, vals, plan, near, send, keep, acc, table):
    acc[...] = jnp.zeros_like(acc)
    for part, side in enumerate(sides(lax.axis_index("band"))):
        for j in range(blocks):
            for piece in range(shares.pieces):
                table[(part * 2 * blocks + j) * shares.pieces + piece] = shares.slot(
                    part, near[side * blocks + j], piece
                )
    near_slot = lambda s, t, piece: table[t * shares.pieces + piece]
    for_tiles(count, plan, vals, NEAR, [(lambda v, s, t: dot_t(v, x[s]), near_slot)], acc, shares.slots)
    half = shares.slots // 2
    send[...] = acc[:half].reshape(send.shape)
    keep[...] = acc[half : 2 * half].reshape(keep.shape)


def own_kernel(count, shares, x, vals, plan, own, acc):
    acc[...] = jnp.zeros_like(acc)
    forward = (lambda v, s, t: dot(v, x[t]), lambda s, t, piece: shares.slot(0, s, piece))
    backward = (lambda v, s, t: dot_t(v, x[s]), lambda s, t, piece: shares.slot(1, t, piece))
    for_tiles(count, plan, vals, OWN, [forward, backward], acc, shares.slots)
    own[...] = acc[: shares.slots]


def remote_kernel(
    count, blocks, shares, vals, plan, near, perm, own, pair, pair2, other, other2, head_x, heads, came, send, keep, acc, xw, table
):
    half_blocks = blocks // 2
    tile = xw.shape[1]
    core = lax.axis_index("level") & 1
    for j in range(half_blocks):
        for at, (mine, swapped) in enumerate(((pair, pair2), (other, other2))):
            xw[at * blocks + core * half_blocks + j] = mine[j * tile : (j + 1) * tile]
            xw[at * blocks + (1 - core) * half_blocks + j] = swapped[j * tile : (j + 1) * tile]
    for j in range(HEADB):
        xw[2 * blocks + j] = head_x[j]
        table[3 * blocks + j] = 2 * blocks + j
    for part, side in enumerate(sides(lax.axis_index("band"))):
        for j in range(blocks):
            table[part * 2 * blocks + j] = side * blocks + near[side * blocks + j]
    acc[: shares.slots] = own[...]
    forward = (lambda v, s, t: dot(v, xw[table[s]]), lambda s, t, piece: shares.slot(0, t, piece))
    backward = (lambda v, s, t: dot_t(v, xw[2 * blocks + t]), lambda s, t, piece: shares.slot(1, s, piece))
    for_tiles(count, plan, vals, REMOTE, [forward], acc, shares.slots)
    for_tiles(count, plan, vals, HEAD_ROW, [backward], acc, shares.slots)

    @pl.when(lax.axis_index("band") == 0)
    def _():
        for part in range(2):
            for h in range(HEADB):
                value = heads[part * HEADB + h] + get_coded(came, part * HEADB + h)
                for piece in range(shares.pieces):
                    acc[shares.slot(part, perm[h], piece)] += value[piece * shares.unit : (piece + 1) * shares.unit]

    half = shares.slots // 2
    send[...] = acc[:half].reshape(send.shape)
    keep[...] = acc[half : 2 * half].reshape(keep.shape)


def split_kernel(bit, coded_in, had, came, send, keep):
    mine = (lax.axis_index("level") >> bit) & 1
    parts, m, share, width = had.shape
    for part in range(parts):
        for i in range(m // 2):
            for half in range(2):
                j = 2 * i + (mine if half else 1 - mine)
                came_value = get_coded(came, part * m + j) if coded_in else came[part, j]
                value = had[part, j] + came_value
                if half:
                    keep[part, i] = value
                else:
                    put_coded(send, part * (m // 2) + i, value)


def edge_kernel(coded_in, had, came, relayed, direct):
    odd = lax.axis_index("band") & 1
    for side, part in ((0, 1 - odd), (1, odd)):
        came_value = get_coded(came, part) if coded_in else came[part, 0]
        value = had[part, 0] + came_value
        if side:
            put_coded(relayed, 0, value)
        else:
            direct[0] = value


def relay_kernel(direct, came, out):
    put_coded(out, 0, direct[0] + get_coded(came, 0))


def last_kernel(coded_in, had, came, from_near, forward, backward):
    came_values = [get_coded(came, part) if coded_in else came[part, 0] for part in range(2)]
    forward[0] = (had[0, 0] + came_values[0]).astype(forward.dtype)
    backward[0] = (had[1, 0] + came_values[1] + get_coded(from_near, 0)).astype(backward.dtype)


def over_levels(send, keep, levels, after=()):
    bit, coded = 0, False
    parts, m, share, width = keep.shape
    while True:
        pairs = [(i, i ^ (1 << bit)) for i in range(levels)]
        came = lax.ppermute(send, "level", pairs)
        if m == 1:
            return keep, came, coded
        bit += 1
        send, keep = call(
            functools.partial(split_kernel, bit, coded),
            (array((parts * (m // 2), share + GROUPS, width), I16), array((parts, m // 2, share, width))),
            (keep, came),
            after=after,
        )
        coded = True
        m //= 2


def on_device(features, block_perm, tile_rows, tile_cols, tile_vals):
    rdev, width = features.shape
    blocks = block_perm.shape[2]
    tile = tile_vals.shape[2]
    count = tile_vals.shape[1]
    levels = lax.axis_size("level")
    bands = lax.axis_size("band")
    band = lax.axis_index("band")
    cores = [(i, i ^ 1) for i in range(levels)]
    pairs = [(i, i ^ 1) for i in range(bands)]
    outward = [(i, i + 2 if i % 2 else i - 2) for i in range(bands)]
    outward = [(i, j) for i, j in outward if 0 <= j < bands]
    inward = [(j, i) for i, j in outward]
    shares = Shares(levels, rdev, tile, 2)
    share, m, unit = shares.share, shares.m, shares.unit

    perm = block_perm[0, 0]
    vals = tile_vals[0]
    x = features.reshape(blocks, tile, width)
    half = lax.dynamic_slice_in_dim(features, (lax.axis_index("level") & 1) * (rdev // 2), rdev // 2, 0)
    order_row = jnp.pad(perm.astype(features.dtype)[None], ((0, PAD_ROWS - 1), (0, width - blocks)))
    mine = jnp.concatenate([half, order_row])
    pair_x = lax.ppermute(mine, "band", pairs)
    other_x = lax.ppermute(pair_x, "band", inward)
    pair_x2 = lax.ppermute(pair_x, "level", cores)
    other_x2 = lax.ppermute(other_x, "level", cores)
    near = jnp.concatenate([a[rdev // 2, :blocks] for a in (pair_x, other_x)]).astype(jnp.int32)

    coded_heads = array((2 * HEADB, tile + GROUPS, width), I16)
    plain_heads = array((2 * HEADB, tile, width))
    in_hbm = lambda a: pltpu.with_memory_space_constraint(a, pltpu.HBM)
    plan, coded, heads, xh, x, vals = call(
        functools.partial(heads_out_kernel, count, blocks),
        (
            array((5 * count + 5,), jnp.int32),
            coded_heads,
            plain_heads,
            array((HEADB, tile, width), x.dtype),
            pltpu.VMEM(x.shape, x.dtype),
            pltpu.VMEM(vals.shape, vals.dtype),
        ),
        tuple(in_hbm(a) for a in (tile_rows, tile_cols, block_perm, x, vals)),
        (
            pltpu.VMEM((2 * HEADB + 1, tile, width), F32),
            pltpu.SMEM(tile_rows.shape, jnp.int32),
            pltpu.SMEM(tile_cols.shape, jnp.int32),
            pltpu.SMEM(block_perm.shape, jnp.int32),
            pltpu.SemaphoreType.DMA((5,)),
        ),
        in_hbm=5,
    )
    x, vals = (pltpu.with_memory_space_constraint(a, pltpu.VMEM) for a in (x, vals))

    half_shape = array((2, m, share, width))
    halo_out = functools.partial(
        call,
        functools.partial(halo_out_kernel, count, blocks, shares),
        (half_shape, half_shape),
        (x, vals, plan, near),
        (
            pltpu.VMEM((shares.slots + 1, unit, width), F32),
            pltpu.SMEM((3 * blocks * shares.pieces,), jnp.int32),
        ),
    )
    own = call(
        functools.partial(own_kernel, count, shares),
        (array((shares.slots, unit, width)),),
        (x, vals, plan),
        (pltpu.VMEM((shares.slots + 1, unit, width), F32),),
    )[0]

    order = [1 << i for i in range(1, bands.bit_length() - 1)] + [1]
    halo_send = halo_keep = None
    fences = [(pair_x,), (own,)] + [()] * bands
    done = 0
    for at, bit in enumerate(order):
        step = bands >> (at + 1)
        senders = [i for i in range(bands) if i & bit and not i & done]
        done |= bit
        came = lax.ppermute(coded, "band", [(i, i - bit) for i in senders])
        got = lax.ppermute(xh, "band", [(i, i + step) for i in range(0, bands, 2 * step)])
        if at == 1:
            halo_send, halo_keep = halo_out(after=(coded, got))
        if bit != order[-1]:
            coded, heads, *passed = call(
                heads_add_kernel,
                (coded_heads, plain_heads),
                (heads, came),
                after=fences[at],
                through=(halo_send,) if at == 1 else (),
            )
            halo_send = passed[0] if passed else halo_send
        xh = call(
            functools.partial(heads_take_kernel, step), (array(xh.shape, xh.dtype),), (xh, got), after=(coded,)
        )[0]
    halo_had, halo_came, halo_coded = over_levels(halo_send, halo_keep, levels)

    send, keep = call(
        functools.partial(remote_kernel, count, blocks, shares),
        (half_shape, half_shape),
        (vals, plan, near, perm, own, pair_x, pair_x2, other_x, other_x2, xh, heads, came),
        (
            pltpu.VMEM((shares.slots + 1, unit, width), F32),
            pltpu.VMEM((2 * blocks + HEADB, tile, width), features.dtype),
            pltpu.SMEM((3 * blocks + HEADB,), jnp.int32),
        ),
        after=(halo_came,),
    )
    relayed, direct = call(
        functools.partial(edge_kernel, halo_coded),
        (array((1, share + GROUPS, width), I16), array((1, share, width))),
        (halo_had, halo_came),
    )
    had, came, was_coded = over_levels(send, keep, levels, after=(direct,))
    relayed = lax.ppermute(relayed, "band", outward)
    to_pair = call(relay_kernel, (array((1, share + GROUPS, width), I16),), (direct, relayed))[0]
    from_near = lax.ppermute(to_pair, "band", pairs)

    out = array((1, share, width), jnp.bfloat16)
    forward, backward = call(functools.partial(last_kernel, was_coded), (out, out), (had, came, from_near))
    return forward, backward


def solution(mesh):
    return jax.shard_map(
        on_device,
        mesh=mesh,
        in_specs=(
            P("band", None),
            P("level", "band", None),
            P("level", "band"),
            P("level", "band"),
            P("level", "band", None, None),
        ),
        out_specs=(P("band", "level", None), P("band", "level", None)),
        check_vma=False,
    )
```

```python
import functools
import math

import jax
import jax.numpy as jnp
from jax import lax
from jax.experimental import pallas as pl
from jax.experimental.pallas import tpu as pltpu
from jax.sharding import PartitionSpec as P

HEADB = 2
GROUPS = 16
UNROLL = 8
PAD_ROWS = 128
VMEM_LIMIT = 24 * 2**20
F32 = jnp.float32
I16 = jnp.int16
VMEM = pl.BlockSpec(memory_space=pltpu.VMEM)
ANY = pl.BlockSpec(memory_space=pl.ANY)
HBM = pl.BlockSpec(memory_space=pltpu.HBM)
SMEM = pl.BlockSpec(memory_space=pltpu.SMEM)


def call(kernel, outs, ins, scratch=(), after=(), in_hbm=0, through=()):
    bytes_moved = sum(math.prod(a.shape) * a.dtype.itemsize for a in (*outs, *ins))

    def body(*refs):
        outputs = len(ins) + len(after) + len(through)
        kernel(*refs[: len(ins)], *refs[outputs : outputs + len(outs)], *refs[outputs + len(outs) + len(through) :])

    return pl.pallas_call(
        body,
        out_shape=[*outs, *(array(a.shape, a.dtype) for a in through)],
        in_specs=[HBM] * in_hbm + [SMEM if a.ndim == 1 else VMEM for a in ins[in_hbm:]] + [ANY] * len((*after, *through)),
        out_specs=[SMEM if len(a.shape) == 1 else VMEM for a in outs] + [ANY] * len(through),
        input_output_aliases={len(ins) + len(after) + i: len(outs) + i for i in range(len(through))},
        scratch_shapes=list(scratch),
        compiler_params=pltpu.CompilerParams(vmem_limit_bytes=VMEM_LIMIT),
        cost_estimate=pl.CostEstimate(flops=0, bytes_accessed=bytes_moved, transcendentals=0),
    )(*ins, *after, *through)


def array(shape, dtype=F32):
    return jax.ShapeDtypeStruct(tuple(shape), dtype)


def encode(value):
    rows, width = value.shape
    grouped = value.reshape(GROUPS, rows // GROUPS, width)
    largest = jnp.maximum(jnp.max(jnp.abs(grouped), axis=1), 1e-30)
    power = jnp.ceil(jnp.log2(largest))
    scaled = jnp.round(grouped * jnp.exp2(15.0 - power)[:, None, :])
    codes = jnp.clip(scaled, -32767.0, 32767.0).astype(jnp.int32).astype(I16)
    return codes.reshape(rows, width), power.astype(jnp.int32).astype(I16)


def put_coded(ref, index, value):
    rows = value.shape[0]
    codes, power = encode(value)
    ref[index, :rows, :] = codes
    ref[index, rows:, :] = power


def get_coded(ref, index):
    rows, width = ref.shape[-2] - GROUPS, ref.shape[-1]
    codes = ref[index, :rows, :].astype(jnp.int32).astype(F32)
    power = ref[index, rows:, :].astype(jnp.int32).astype(F32)
    grouped = codes.reshape(GROUPS, rows // GROUPS, width) * jnp.exp2(power - 15.0)[:, None, :]
    return grouped.reshape(rows, width)


def dot(a, b):
    return jnp.dot(a, b, preferred_element_type=F32)


def dot_t(a, b):
    return lax.dot_general(a, b, (((0,), (0,)), ((), ())), preferred_element_type=F32)


HEAD_ROW, HEAD_COL, NEAR, OWN, REMOTE = range(5)


def packed(k, source, target):
    return k | (source << 8) | (target << 16)


def write_plan(count, blocks, rows, cols, perm, plan):
    low = lax.axis_index("band") * blocks
    n = [jnp.int32(0)] * 5
    for k in range(count):
        row, col = rows[0, k] - low, cols[0, k] - low
        own_row = (row >= 0) & (row < blocks)
        own_col = (col >= 0) & (col < blocks)
        near = (col >= -blocks) & (col < 2 * blocks)
        x_row = perm[0, 0, jnp.clip(row, 0, blocks - 1)]
        x_col = perm[0, 0, jnp.clip(col, 0, blocks - 1)]
        near_at = jnp.where(near, col + blocks, 3 * blocks + cols[0, k])
        for which, chosen, source, target in (
            (HEAD_ROW, ~own_row, x_col, rows[0, k]),
            (HEAD_COL, own_row & ~near, x_row, HEADB + cols[0, k]),
            (NEAR, own_row & near & ~own_col, x_row, near_at),
            (OWN, own_row & own_col, x_row, x_col),
            (REMOTE, own_row & ~own_col, near_at, x_row),
        ):
            plan[which * count + n[which]] = packed(k, source, target)
            n[which] = n[which] + chosen.astype(jnp.int32)
    for which in range(5):
        plan[5 * count + which] = n[which]


def for_tiles(count, plan, vals, which, jobs, acc, trash):
    n = plan[5 * count + which]
    unit = acc.shape[1]

    def step(i, carry):
        entries = []
        for u in range(UNROLL):
            real = i * UNROLL + u < n
            e = plan[which * count + jnp.minimum(i * UNROLL + u, n - 1)]
            entries.append((real, e & 255, (e >> 8) & 255, e >> 16))
        products = [[product(vals[k], s, t) for product, _ in jobs] for _, k, s, t in entries]
        for values, (real, _, s, t) in zip(products, entries):
            for value, (_, place) in zip(values, jobs):
                for piece in range(value.shape[0] // unit):
                    slot = jnp.where(real, place(s, t, piece), trash)
                    acc[slot] += value[piece * unit : (piece + 1) * unit]
        return carry

    lax.fori_loop(0, (n + UNROLL - 1) // UNROLL, step, 0)


class Shares:
    def __init__(self, levels, rdev, tile, parts):
        self.share = rdev // levels
        self.unit = min(tile, self.share)
        self.per = self.share // self.unit
        self.m = levels // 2
        self.parts = parts
        self.tile = tile
        self.pieces = tile // self.unit
        self.slots = 2 * parts * self.m * self.per

    def slot(self, part, block, piece):
        at = block * self.pieces + piece
        owner = at // self.per
        keep = 1 - ((owner ^ lax.axis_index("level")) & 1)
        return ((keep * self.parts + part) * self.m + (owner >> 1)) * self.per + at % self.per


def sides(band):
    odd = band & 1
    return 1 - odd, odd


def heads_out_kernel(count, blocks, rows_hbm, cols_hbm, perm_hbm, x_hbm, vals_hbm, plan, coded, plain, head_x, x, vals, acc, rows, cols, perm, few):
    copies = [
        pltpu.make_async_copy(a, b, few.at[i])
        for i, (a, b) in enumerate(((rows_hbm, rows), (cols_hbm, cols), (perm_hbm, perm), (x_hbm, x), (vals_hbm, vals)))
    ]
    for copy in copies:
        copy.start()
    acc[...] = jnp.zeros_like(acc)
    for copy in copies[:3]:
        copy.wait()
    write_plan(count, blocks, rows, cols, perm, plan)
    copies[3].wait()
    for h in range(HEADB):
        head_x[h] = x[perm[0, 0, h]]
    copies[4].wait()
    target = lambda s, t, piece: t
    for_tiles(count, plan, vals, HEAD_ROW, [(lambda v, s, t: dot(v, x[s]), target)], acc, 2 * HEADB)
    for_tiles(count, plan, vals, HEAD_COL, [(lambda v, s, t: dot_t(v, x[s]), target)], acc, 2 * HEADB)
    for i in range(2 * HEADB):
        plain[i] = acc[i]
        put_coded(coded, i, acc[i])


def heads_take_kernel(step, head_x, head_got, out):
    out[...] = jnp.where(lax.axis_index("band") % (2 * step) == step, head_got[...], head_x[...])


def heads_add_kernel(had, came, coded, plain):
    for i in range(had.shape[0]):
        value = had[i] + get_coded(came, i)
        plain[i] = value
        put_coded(coded, i, value)


def halo_out_kernel(count, blocks, shares, x, vals, plan, near, send, keep, acc, table):
    acc[...] = jnp.zeros_like(acc)
    for part, side in enumerate(sides(lax.axis_index("band"))):
        for j in range(blocks):
            for piece in range(shares.pieces):
                table[(part * 2 * blocks + j) * shares.pieces + piece] = shares.slot(
                    part, near[side * blocks + j], piece
                )
    near_slot = lambda s, t, piece: table[t * shares.pieces + piece]
    for_tiles(count, plan, vals, NEAR, [(lambda v, s, t: dot_t(v, x[s]), near_slot)], acc, shares.slots)
    half = shares.slots // 2
    send[...] = acc[:half].reshape(send.shape)
    keep[...] = acc[half : 2 * half].reshape(keep.shape)


def own_kernel(count, shares, x, vals, plan, own, acc):
    acc[...] = jnp.zeros_like(acc)
    forward = (lambda v, s, t: dot(v, x[t]), lambda s, t, piece: shares.slot(0, s, piece))
    backward = (lambda v, s, t: dot_t(v, x[s]), lambda s, t, piece: shares.slot(1, t, piece))
    for_tiles(count, plan, vals, OWN, [forward, backward], acc, shares.slots)
    own[...] = acc[: shares.slots]


def remote_kernel(
    count, blocks, shares, vals, plan, near, perm, own, pair, pair2, other, other2, head_x, heads, came, send, keep, acc, xw, table
):
    half_blocks = blocks // 2
    tile = xw.shape[1]
    core = lax.axis_index("level") & 1
    for j in range(half_blocks):
        for at, (mine, swapped) in enumerate(((pair, pair2), (other, other2))):
            xw[at * blocks + core * half_blocks + j] = mine[j * tile : (j + 1) * tile]
            xw[at * blocks + (1 - core) * half_blocks + j] = swapped[j * tile : (j + 1) * tile]
    for j in range(HEADB):
        xw[2 * blocks + j] = head_x[j]
        table[3 * blocks + j] = 2 * blocks + j
    for part, side in enumerate(sides(lax.axis_index("band"))):
        for j in range(blocks):
            table[part * 2 * blocks + j] = side * blocks + near[side * blocks + j]
    acc[: shares.slots] = own[...]
    forward = (lambda v, s, t: dot(v, xw[table[s]]), lambda s, t, piece: shares.slot(0, t, piece))
    backward = (lambda v, s, t: dot_t(v, xw[2 * blocks + t]), lambda s, t, piece: shares.slot(1, s, piece))
    for_tiles(count, plan, vals, REMOTE, [forward], acc, shares.slots)
    for_tiles(count, plan, vals, HEAD_ROW, [backward], acc, shares.slots)

    @pl.when(lax.axis_index("band") == 0)
    def _():
        for part in range(2):
            for h in range(HEADB):
                value = heads[part * HEADB + h] + get_coded(came, part * HEADB + h)
                for piece in range(shares.pieces):
                    acc[shares.slot(part, perm[h], piece)] += value[piece * shares.unit : (piece + 1) * shares.unit]

    half = shares.slots // 2
    send[...] = acc[:half].reshape(send.shape)
    keep[...] = acc[half : 2 * half].reshape(keep.shape)


def split_kernel(bit, coded_in, had, came, send, keep):
    mine = (lax.axis_index("level") >> bit) & 1
    parts, m, share, width = had.shape
    for part in range(parts):
        for i in range(m // 2):
            for half in range(2):
                j = 2 * i + (mine if half else 1 - mine)
                came_value = get_coded(came, part * m + j) if coded_in else came[part, j]
                value = had[part, j] + came_value
                if half:
                    keep[part, i] = value
                else:
                    put_coded(send, part * (m // 2) + i, value)


def edge_kernel(coded_in, had, came, relayed, direct):
    odd = lax.axis_index("band") & 1
    for side, part in ((0, 1 - odd), (1, odd)):
        came_value = get_coded(came, part) if coded_in else came[part, 0]
        value = had[part, 0] + came_value
        if side:
            put_coded(relayed, 0, value)
        else:
            direct[0] = value


def relay_kernel(direct, came, out):
    put_coded(out, 0, direct[0] + get_coded(came, 0))


def last_kernel(coded_in, had, came, from_near, forward, backward):
    came_values = [get_coded(came, part) if coded_in else came[part, 0] for part in range(2)]
    forward[0] = (had[0, 0] + came_values[0]).astype(forward.dtype)
    backward[0] = (had[1, 0] + came_values[1] + get_coded(from_near, 0)).astype(backward.dtype)


def over_levels(send, keep, levels, after=()):
    bit, coded = 0, False
    parts, m, share, width = keep.shape
    while True:
        pairs = [(i, i ^ (1 << bit)) for i in range(levels)]
        came = lax.ppermute(send, "level", pairs)
        if m == 1:
            return keep, came, coded
        bit += 1
        send, keep = call(
            functools.partial(split_kernel, bit, coded),
            (array((parts * (m // 2), share + GROUPS, width), I16), array((parts, m // 2, share, width))),
            (keep, came),
            after=after,
        )
        coded = True
        m //= 2


def on_device(features, block_perm, tile_rows, tile_cols, tile_vals):
    rdev, width = features.shape
    blocks = block_perm.shape[2]
    tile = tile_vals.shape[2]
    count = tile_vals.shape[1]
    levels = lax.axis_size("level")
    bands = lax.axis_size("band")
    band = lax.axis_index("band")
    cores = [(i, i ^ 1) for i in range(levels)]
    pairs = [(i, i ^ 1) for i in range(bands)]
    outward = [(i, i + 2 if i % 2 else i - 2) for i in range(bands)]
    outward = [(i, j) for i, j in outward if 0 <= j < bands]
    inward = [(j, i) for i, j in outward]
    shares = Shares(levels, rdev, tile, 2)
    share, m, unit = shares.share, shares.m, shares.unit

    perm = block_perm[0, 0]
    vals = tile_vals[0]
    x = features.reshape(blocks, tile, width)
    half = lax.dynamic_slice_in_dim(features, (lax.axis_index("level") & 1) * (rdev // 2), rdev // 2, 0)
    order_row = jnp.pad(perm.astype(features.dtype)[None], ((0, PAD_ROWS - 1), (0, width - blocks)))
    mine = jnp.concatenate([half, order_row])
    pair_x = lax.ppermute(mine, "band", pairs)
    other_x = lax.ppermute(pair_x, "band", inward)
    pair_x2 = lax.ppermute(pair_x, "level", cores)
    other_x2 = lax.ppermute(other_x, "level", cores)
    near = jnp.concatenate([a[rdev // 2, :blocks] for a in (pair_x, other_x)]).astype(jnp.int32)

    coded_heads = array((2 * HEADB, tile + GROUPS, width), I16)
    plain_heads = array((2 * HEADB, tile, width))
    in_hbm = lambda a: pltpu.with_memory_space_constraint(a, pltpu.HBM)
    plan, coded, heads, xh, x, vals = call(
        functools.partial(heads_out_kernel, count, blocks),
        (
            array((5 * count + 5,), jnp.int32),
            coded_heads,
            plain_heads,
            array((HEADB, tile, width), x.dtype),
            pltpu.VMEM(x.shape, x.dtype),
            pltpu.VMEM(vals.shape, vals.dtype),
        ),
        tuple(in_hbm(a) for a in (tile_rows, tile_cols, block_perm, x, vals)),
        (
            pltpu.VMEM((2 * HEADB + 1, tile, width), F32),
            pltpu.SMEM(tile_rows.shape, jnp.int32),
            pltpu.SMEM(tile_cols.shape, jnp.int32),
            pltpu.SMEM(block_perm.shape, jnp.int32),
            pltpu.SemaphoreType.DMA((5,)),
        ),
        in_hbm=5,
    )
    x, vals = (pltpu.with_memory_space_constraint(a, pltpu.VMEM) for a in (x, vals))

    half_shape = array((2, m, share, width))
    halo_out = functools.partial(
        call,
        functools.partial(halo_out_kernel, count, blocks, shares),
        (half_shape, half_shape),
        (x, vals, plan, near),
        (
            pltpu.VMEM((shares.slots + 1, unit, width), F32),
            pltpu.SMEM((3 * blocks * shares.pieces,), jnp.int32),
        ),
    )
    own = call(
        functools.partial(own_kernel, count, shares),
        (array((shares.slots, unit, width)),),
        (x, vals, plan),
        (pltpu.VMEM((shares.slots + 1, unit, width), F32),),
    )[0]

    order = [1 << i for i in range(1, bands.bit_length() - 1)] + [1]
    halo_send = halo_keep = None
    fences = [(pair_x,), (own,)] + [()] * bands
    done = 0
    for at, bit in enumerate(order):
        step = bands >> (at + 1)
        senders = [i for i in range(bands) if i & bit and not i & done]
        done |= bit
        came = lax.ppermute(coded, "band", [(i, i - bit) for i in senders])
        got = lax.ppermute(xh, "band", [(i, i + step) for i in range(0, bands, 2 * step)])
        if at == 1:
            halo_send, halo_keep = halo_out(after=(coded, got))
        if bit != order[-1]:
            coded, heads, *passed = call(
                heads_add_kernel,
                (coded_heads, plain_heads),
                (heads, came),
                after=fences[at],
                through=(halo_send,) if at == 1 else (),
            )
            halo_send = passed[0] if passed else halo_send
        xh = call(
            functools.partial(heads_take_kernel, step), (array(xh.shape, xh.dtype),), (xh, got), after=(coded,)
        )[0]
    halo_had, halo_came, halo_coded = over_levels(halo_send, halo_keep, levels)

    send, keep = call(
        functools.partial(remote_kernel, count, blocks, shares),
        (half_shape, half_shape),
        (vals, plan, near, perm, own, pair_x, pair_x2, other_x, other_x2, xh, heads, came),
        (
            pltpu.VMEM((shares.slots + 1, unit, width), F32),
            pltpu.VMEM((2 * blocks + HEADB, tile, width), features.dtype),
            pltpu.SMEM((3 * blocks + HEADB,), jnp.int32),
        ),
        after=(halo_came,),
    )
    relayed, direct = call(
        functools.partial(edge_kernel, halo_coded),
        (array((1, share + GROUPS, width), I16), array((1, share, width))),
        (halo_had, halo_came),
    )
    had, came, was_coded = over_levels(send, keep, levels, after=(direct,))
    relayed = lax.ppermute(relayed, "band", outward)
    to_pair = call(relay_kernel, (array((1, share + GROUPS, width), I16),), (direct, relayed))[0]
    from_near = lax.ppermute(to_pair, "band", pairs)

    out = array((1, share, width), jnp.bfloat16)
    forward, backward = call(functools.partial(last_kernel, was_coded), (out, out), (had, came, from_near))
    return forward, backward


def solution(mesh):
    return jax.shard_map(
        on_device,
        mesh=mesh,
        in_specs=(
            P("band", None),
            P("level", "band", None),
            P("level", "band"),
            P("level", "band"),
            P("level", "band", None, None),
        ),
        out_specs=(P("band", "level", None), P("band", "level", None)),
        check_vma=False,
    )
```

```python
import functools
import math

import jax
import jax.numpy as jnp
from jax import lax
from jax.experimental import pallas as pl
from jax.experimental.pallas import tpu as pltpu
from jax.sharding import PartitionSpec as P

HEADB = 2
GROUPS = 16
UNROLL = 8
PAD_ROWS = 128
VMEM_LIMIT = 24 * 2**20
F32 = jnp.float32
I16 = jnp.int16
VMEM = pl.BlockSpec(memory_space=pltpu.VMEM)
ANY = pl.BlockSpec(memory_space=pl.ANY)
HBM = pl.BlockSpec(memory_space=pltpu.HBM)
SMEM = pl.BlockSpec(memory_space=pltpu.SMEM)


def call(kernel, outs, ins, scratch=(), after=(), in_hbm=0, through=()):
    bytes_moved = sum(math.prod(a.shape) * a.dtype.itemsize for a in (*outs, *ins))

    def body(*refs):
        outputs = len(ins) + len(after) + len(through)
        kernel(*refs[: len(ins)], *refs[outputs : outputs + len(outs)], *refs[outputs + len(outs) + len(through) :])

    return pl.pallas_call(
        body,
        out_shape=[*outs, *(array(a.shape, a.dtype) for a in through)],
        in_specs=[HBM] * in_hbm + [SMEM if a.ndim == 1 else VMEM for a in ins[in_hbm:]] + [ANY] * len((*after, *through)),
        out_specs=[SMEM if len(a.shape) == 1 else VMEM for a in outs] + [ANY] * len(through),
        input_output_aliases={len(ins) + len(after) + i: len(outs) + i for i in range(len(through))},
        scratch_shapes=list(scratch),
        compiler_params=pltpu.CompilerParams(vmem_limit_bytes=VMEM_LIMIT),
        cost_estimate=pl.CostEstimate(flops=0, bytes_accessed=bytes_moved, transcendentals=0),
    )(*ins, *after, *through)


def array(shape, dtype=F32):
    return jax.ShapeDtypeStruct(tuple(shape), dtype)


def encode(value):
    rows, width = value.shape
    grouped = value.reshape(GROUPS, rows // GROUPS, width)
    largest = jnp.maximum(jnp.max(jnp.abs(grouped), axis=1), 1e-30)
    power = jnp.ceil(jnp.log2(largest))
    scaled = jnp.round(grouped * jnp.exp2(15.0 - power)[:, None, :])
    codes = jnp.clip(scaled, -32767.0, 32767.0).astype(jnp.int32).astype(I16)
    return codes.reshape(rows, width), power.astype(jnp.int32).astype(I16)


def put_coded(ref, index, value):
    rows = value.shape[0]
    codes, power = encode(value)
    ref[index, :rows, :] = codes
    ref[index, rows:, :] = power


def get_coded(ref, index):
    rows, width = ref.shape[-2] - GROUPS, ref.shape[-1]
    codes = ref[index, :rows, :].astype(jnp.int32).astype(F32)
    power = ref[index, rows:, :].astype(jnp.int32).astype(F32)
    grouped = codes.reshape(GROUPS, rows // GROUPS, width) * jnp.exp2(power - 15.0)[:, None, :]
    return grouped.reshape(rows, width)


def dot(a, b):
    return jnp.dot(a, b, preferred_element_type=F32)


def dot_t(a, b):
    return lax.dot_general(a, b, (((0,), (0,)), ((), ())), preferred_element_type=F32)


HEAD_ROW, HEAD_COL, NEAR, OWN, REMOTE = range(5)


def packed(k, source, target):
    return k | (source << 8) | (target << 16)


def write_plan(count, blocks, rows, cols, perm, plan):
    low = lax.axis_index("band") * blocks
    n = [jnp.int32(0)] * 5
    for k in range(count):
        row, col = rows[0, k] - low, cols[0, k] - low
        own_row = (row >= 0) & (row < blocks)
        own_col = (col >= 0) & (col < blocks)
        near = (col >= -blocks) & (col < 2 * blocks)
        x_row = perm[0, 0, jnp.clip(row, 0, blocks - 1)]
        x_col = perm[0, 0, jnp.clip(col, 0, blocks - 1)]
        near_at = jnp.where(near, col + blocks, 3 * blocks + cols[0, k])
        for which, chosen, source, target in (
            (HEAD_ROW, ~own_row, x_col, rows[0, k]),
            (HEAD_COL, own_row & ~near, x_row, HEADB + cols[0, k]),
            (NEAR, own_row & near & ~own_col, x_row, near_at),
            (OWN, own_row & own_col, x_row, x_col),
            (REMOTE, own_row & ~own_col, near_at, x_row),
        ):
            plan[which * count + n[which]] = packed(k, source, target)
            n[which] = n[which] + chosen.astype(jnp.int32)
    for which in range(5):
        plan[5 * count + which] = n[which]


def for_tiles(count, plan, vals, which, jobs, acc, trash):
    n = plan[5 * count + which]
    unit = acc.shape[1]

    def step(i, carry):
        entries = []
        for u in range(UNROLL):
            real = i * UNROLL + u < n
            e = plan[which * count + jnp.minimum(i * UNROLL + u, n - 1)]
            entries.append((real, e & 255, (e >> 8) & 255, e >> 16))
        products = [[product(vals[k], s, t) for product, _ in jobs] for _, k, s, t in entries]
        for values, (real, _, s, t) in zip(products, entries):
            for value, (_, place) in zip(values, jobs):
                for piece in range(value.shape[0] // unit):
                    slot = jnp.where(real, place(s, t, piece), trash)
                    acc[slot] += value[piece * unit : (piece + 1) * unit]
        return carry

    lax.fori_loop(0, (n + UNROLL - 1) // UNROLL, step, 0)


class Shares:
    def __init__(self, levels, rdev, tile, parts):
        self.share = rdev // levels
        self.unit = min(tile, self.share)
        self.per = self.share // self.unit
        self.m = levels // 2
        self.parts = parts
        self.tile = tile
        self.pieces = tile // self.unit
        self.slots = 2 * parts * self.m * self.per

    def slot(self, part, block, piece):
        at = block * self.pieces + piece
        owner = at // self.per
        keep = 1 - ((owner ^ lax.axis_index("level")) & 1)
        return ((keep * self.parts + part) * self.m + (owner >> 1)) * self.per + at % self.per


def sides(band):
    odd = band & 1
    return 1 - odd, odd


def heads_out_kernel(count, blocks, rows_hbm, cols_hbm, perm_hbm, x_hbm, vals_hbm, plan, coded, plain, head_x, x, vals, acc, rows, cols, perm, few):
    copies = [
        pltpu.make_async_copy(a, b, few.at[i])
        for i, (a, b) in enumerate(((rows_hbm, rows), (cols_hbm, cols), (perm_hbm, perm), (x_hbm, x), (vals_hbm, vals)))
    ]
    for copy in copies:
        copy.start()
    acc[...] = jnp.zeros_like(acc)
    for copy in copies[:3]:
        copy.wait()
    write_plan(count, blocks, rows, cols, perm, plan)
    copies[3].wait()
    for h in range(HEADB):
        head_x[h] = x[perm[0, 0, h]]
    copies[4].wait()
    target = lambda s, t, piece: t
    for_tiles(count, plan, vals, HEAD_ROW, [(lambda v, s, t: dot(v, x[s]), target)], acc, 2 * HEADB)
    for_tiles(count, plan, vals, HEAD_COL, [(lambda v, s, t: dot_t(v, x[s]), target)], acc, 2 * HEADB)
    for i in range(2 * HEADB):
        plain[i] = acc[i]
        put_coded(coded, i, acc[i])


def heads_take_kernel(step, head_x, head_got, out):
    out[...] = jnp.where(lax.axis_index("band") % (2 * step) == step, head_got[...], head_x[...])


def heads_add_kernel(had, came, coded, plain):
    for i in range(had.shape[0]):
        value = had[i] + get_coded(came, i)
        plain[i] = value
        put_coded(coded, i, value)


def halo_out_kernel(count, blocks, shares, x, vals, plan, near, send, keep, acc, table):
    acc[...] = jnp.zeros_like(acc)
    for part, side in enumerate(sides(lax.axis_index("band"))):
        for j in range(blocks):
            for piece in range(shares.pieces):
                table[(part * 2 * blocks + j) * shares.pieces + piece] = shares.slot(
                    part, near[side * blocks + j], piece
                )
    near_slot = lambda s, t, piece: table[t * shares.pieces + piece]
    for_tiles(count, plan, vals, NEAR, [(lambda v, s, t: dot_t(v, x[s]), near_slot)], acc, shares.slots)
    half = shares.slots // 2
    send[...] = acc[:half].reshape(send.shape)
    keep[...] = acc[half : 2 * half].reshape(keep.shape)


def own_kernel(count, shares, x, vals, plan, own, acc):
    acc[...] = jnp.zeros_like(acc)
    forward = (lambda v, s, t: dot(v, x[t]), lambda s, t, piece: shares.slot(0, s, piece))
    backward = (lambda v, s, t: dot_t(v, x[s]), lambda s, t, piece: shares.slot(1, t, piece))
    for_tiles(count, plan, vals, OWN, [forward, backward], acc, shares.slots)
    own[...] = acc[: shares.slots]


def remote_kernel(
    count, blocks, shares, vals, plan, near, perm, own, pair, pair2, other, other2, head_x, heads, came, send, keep, acc, xw, table
):
    half_blocks = blocks // 2
    tile = xw.shape[1]
    core = lax.axis_index("level") & 1
    for j in range(half_blocks):
        for at, (mine, swapped) in enumerate(((pair, pair2), (other, other2))):
            xw[at * blocks + core * half_blocks + j] = mine[j * tile : (j + 1) * tile]
            xw[at * blocks + (1 - core) * half_blocks + j] = swapped[j * tile : (j + 1) * tile]
    for j in range(HEADB):
        xw[2 * blocks + j] = head_x[j]
        table[3 * blocks + j] = 2 * blocks + j
    for part, side in enumerate(sides(lax.axis_index("band"))):
        for j in range(blocks):
            table[part * 2 * blocks + j] = side * blocks + near[side * blocks + j]
    acc[: shares.slots] = own[...]
    forward = (lambda v, s, t: dot(v, xw[table[s]]), lambda s, t, piece: shares.slot(0, t, piece))
    backward = (lambda v, s, t: dot_t(v, xw[2 * blocks + t]), lambda s, t, piece: shares.slot(1, s, piece))
    for_tiles(count, plan, vals, REMOTE, [forward], acc, shares.slots)
    for_tiles(count, plan, vals, HEAD_ROW, [backward], acc, shares.slots)

    @pl.when(lax.axis_index("band") == 0)
    def _():
        for part in range(2):
            for h in range(HEADB):
                value = heads[part * HEADB + h] + get_coded(came, part * HEADB + h)
                for piece in range(shares.pieces):
                    acc[shares.slot(part, perm[h], piece)] += value[piece * shares.unit : (piece + 1) * shares.unit]

    half = shares.slots // 2
    send[...] = acc[:half].reshape(send.shape)
    keep[...] = acc[half : 2 * half].reshape(keep.shape)


def split_kernel(bit, coded_in, had, came, send, keep):
    mine = (lax.axis_index("level") >> bit) & 1
    parts, m, share, width = had.shape
    for part in range(parts):
        for i in range(m // 2):
            for half in range(2):
                j = 2 * i + (mine if half else 1 - mine)
                came_value = get_coded(came, part * m + j) if coded_in else came[part, j]
                value = had[part, j] + came_value
                if half:
                    keep[part, i] = value
                else:
                    put_coded(send, part * (m // 2) + i, value)


def edge_kernel(coded_in, had, came, relayed, direct):
    odd = lax.axis_index("band") & 1
    for side, part in ((0, 1 - odd), (1, odd)):
        came_value = get_coded(came, part) if coded_in else came[part, 0]
        value = had[part, 0] + came_value
        if side:
            put_coded(relayed, 0, value)
        else:
            direct[0] = value


def relay_kernel(direct, came, out):
    put_coded(out, 0, direct[0] + get_coded(came, 0))


def last_kernel(coded_in, had, came, from_near, forward, backward):
    came_values = [get_coded(came, part) if coded_in else came[part, 0] for part in range(2)]
    forward[0] = (had[0, 0] + came_values[0]).astype(forward.dtype)
    backward[0] = (had[1, 0] + came_values[1] + get_coded(from_near, 0)).astype(backward.dtype)


def over_levels(send, keep, levels, after=()):
    bit, coded = 0, False
    parts, m, share, width = keep.shape
    while True:
        pairs = [(i, i ^ (1 << bit)) for i in range(levels)]
        came = lax.ppermute(send, "level", pairs)
        if m == 1:
            return keep, came, coded
        bit += 1
        send, keep = call(
            functools.partial(split_kernel, bit, coded),
            (array((parts * (m // 2), share + GROUPS, width), I16), array((parts, m // 2, share, width))),
            (keep, came),
            after=after,
        )
        coded = True
        m //= 2


def on_device(features, block_perm, tile_rows, tile_cols, tile_vals):
    rdev, width = features.shape
    blocks = block_perm.shape[2]
    tile = tile_vals.shape[2]
    count = tile_vals.shape[1]
    levels = lax.axis_size("level")
    bands = lax.axis_size("band")
    band = lax.axis_index("band")
    cores = [(i, i ^ 1) for i in range(levels)]
    pairs = [(i, i ^ 1) for i in range(bands)]
    outward = [(i, i + 2 if i % 2 else i - 2) for i in range(bands)]
    outward = [(i, j) for i, j in outward if 0 <= j < bands]
    inward = [(j, i) for i, j in outward]
    shares = Shares(levels, rdev, tile, 2)
    share, m, unit = shares.share, shares.m, shares.unit

    perm = block_perm[0, 0]
    vals = tile_vals[0]
    x = features.reshape(blocks, tile, width)
    half = lax.dynamic_slice_in_dim(features, (lax.axis_index("level") & 1) * (rdev // 2), rdev // 2, 0)
    order_row = jnp.pad(perm.astype(features.dtype)[None], ((0, PAD_ROWS - 1), (0, width - blocks)))
    mine = jnp.concatenate([half, order_row])
    pair_x = lax.ppermute(mine, "band", pairs)
    other_x = lax.ppermute(pair_x, "band", inward)
    pair_x2 = lax.ppermute(pair_x, "level", cores)
    other_x2 = lax.ppermute(other_x, "level", cores)
    near = jnp.concatenate([a[rdev // 2, :blocks] for a in (pair_x, other_x)]).astype(jnp.int32)

    coded_heads = array((2 * HEADB, tile + GROUPS, width), I16)
    plain_heads = array((2 * HEADB, tile, width))
    in_hbm = lambda a: pltpu.with_memory_space_constraint(a, pltpu.HBM)
    plan, coded, heads, xh, x, vals = call(
        functools.partial(heads_out_kernel, count, blocks),
        (
            array((5 * count + 5,), jnp.int32),
            coded_heads,
            plain_heads,
            array((HEADB, tile, width), x.dtype),
            pltpu.VMEM(x.shape, x.dtype),
            pltpu.VMEM(vals.shape, vals.dtype),
        ),
        tuple(in_hbm(a) for a in (tile_rows, tile_cols, block_perm, x, vals)),
        (
            pltpu.VMEM((2 * HEADB + 1, tile, width), F32),
            pltpu.SMEM(tile_rows.shape, jnp.int32),
            pltpu.SMEM(tile_cols.shape, jnp.int32),
            pltpu.SMEM(block_perm.shape, jnp.int32),
            pltpu.SemaphoreType.DMA((5,)),
        ),
        in_hbm=5,
    )
    x, vals = (pltpu.with_memory_space_constraint(a, pltpu.VMEM) for a in (x, vals))

    half_shape = array((2, m, share, width))
    halo_out = functools.partial(
        call,
        functools.partial(halo_out_kernel, count, blocks, shares),
        (half_shape, half_shape),
        (x, vals, plan, near),
        (
            pltpu.VMEM((shares.slots + 1, unit, width), F32),
            pltpu.SMEM((3 * blocks * shares.pieces,), jnp.int32),
        ),
    )
    own = call(
        functools.partial(own_kernel, count, shares),
        (array((shares.slots, unit, width)),),
        (x, vals, plan),
        (pltpu.VMEM((shares.slots + 1, unit, width), F32),),
    )[0]

    order = [1 << i for i in range(1, bands.bit_length() - 1)] + [1]
    halo_send = halo_keep = None
    fences = [(pair_x,), (own,)] + [()] * bands
    done = 0
    for at, bit in enumerate(order):
        step = bands >> (at + 1)
        senders = [i for i in range(bands) if i & bit and not i & done]
        done |= bit
        came = lax.ppermute(coded, "band", [(i, i - bit) for i in senders])
        got = lax.ppermute(xh, "band", [(i, i + step) for i in range(0, bands, 2 * step)])
        if at == 1:
            halo_send, halo_keep = halo_out(after=(coded,))
        if bit != order[-1]:
            coded, heads, *passed = call(
                heads_add_kernel,
                (coded_heads, plain_heads),
                (heads, came),
                after=(*fences[at], got) if at == 1 else fences[at],
                through=(halo_send,) if at == 1 else (),
            )
            halo_send = passed[0] if passed else halo_send
        xh = call(
            functools.partial(heads_take_kernel, step), (array(xh.shape, xh.dtype),), (xh, got), after=(coded,)
        )[0]
    halo_had, halo_came, halo_coded = over_levels(halo_send, halo_keep, levels)

    send, keep = call(
        functools.partial(remote_kernel, count, blocks, shares),
        (half_shape, half_shape),
        (vals, plan, near, perm, own, pair_x, pair_x2, other_x, other_x2, xh, heads, came),
        (
            pltpu.VMEM((shares.slots + 1, unit, width), F32),
            pltpu.VMEM((2 * blocks + HEADB, tile, width), features.dtype),
            pltpu.SMEM((3 * blocks + HEADB,), jnp.int32),
        ),
        after=(halo_came,),
    )
    relayed, direct = call(
        functools.partial(edge_kernel, halo_coded),
        (array((1, share + GROUPS, width), I16), array((1, share, width))),
        (halo_had, halo_came),
    )
    had, came, was_coded = over_levels(send, keep, levels, after=(direct,))
    relayed = lax.ppermute(relayed, "band", outward)
    to_pair = call(relay_kernel, (array((1, share + GROUPS, width), I16),), (direct, relayed))[0]
    from_near = lax.ppermute(to_pair, "band", pairs)

    out = array((1, share, width), jnp.bfloat16)
    forward, backward = call(functools.partial(last_kernel, was_coded), (out, out), (had, came, from_near))
    return forward, backward


def solution(mesh):
    return jax.shard_map(
        on_device,
        mesh=mesh,
        in_specs=(
            P("band", None),
            P("level", "band", None),
            P("level", "band"),
            P("level", "band"),
            P("level", "band", None, None),
        ),
        out_specs=(P("band", "level", None), P("band", "level", None)),
        check_vma=False,
    )
```
